256 devices in a mesh: shard: 32 (over x, y, core), tensor: 8 (over z).
Axes of the slice: x: 4, y: 4, z: 8, core: 2. Of those that a mesh axis runs over, the one named last changes fastest.
Arguments:
- cand_rows: bfloat16 [65536, 1024], P('shard'), may hold values from -24 to 24
- proj_weight: bfloat16 [1024, 4, 1024], P(None, None, 'tensor'), may hold values from -0.1875 to 0.1875
- out_weight: bfloat16 [1024, 1024], P('tensor'), may hold values from -0.5 to 0.5
- self_bias: float32 [16], P('tensor'), may hold values from 1 to 4
- history_cache: bfloat16 [64, 2048, 2, 1024], P('shard', None, None, 'tensor'), may hold values from -6 to 6
- history_length: int32 [64], replicated, may hold values from 1 to 2048, 65536 in all
- candidate_slot: int32 [65536, 1], P('shard'), may hold values from 0 to 63; in each aligned block of 2048 rows (0 to 2047, 2048 to 4095, ...) at most 64 rows name the same one
- hot_slot: int32 [32], replicated, may hold values from 0 to 1
Outputs:
- layer_out: bfloat16 [65536, 1024], P('shard', 'tensor')
The draws below stay inside these ranges and needn't reach their ends.
Inputs may be any that keep to these rules, and one draw needn't show every extreme that they name: `candidate_slot`: every cache slot is named by some row; within the rows of one shard index no slot is named more than 64 times, and some shard index names some slot exactly 64 times.
All inputs are finite; a program needn't handle non-finite values.
Results may differ from the reference program's by a relative error of at most 0.0062.
Values may be sent and summed in bfloat16 or wider, within the bound.
No kernel may reach another device: no remote copies, remote signals or barrier semaphores. Data moves between devices by JAX's collectives and lax.ppermute only.
A program may use at most 64 MiB of HBM per device.

```python
import math
import jax
import jax.numpy as jnp
import numpy as np
from jax import lax

D = 1024
H = 16
DH = 64
R_DEV = 2
C_DEV = 2048
HMAX = 2048
KBLK = 512
HD = 1024
REQS = 64
CANDS = 65536
CAPS = 64
N_SHARD = 32


def draw_cand_rows(key, part):
    key = jax.random.fold_in(key, 7)
    first, second, third = jax.random.split(key, 3)
    row_scale = jnp.exp(jax.random.uniform(second, (CANDS, 1), jnp.float32, math.log(0.3), math.log(3.0)))
    col_scale = jnp.exp(jax.random.uniform(third, (1, D), jnp.float32, math.log(0.5), math.log(2.0)))
    base_rows = jnp.clip(jax.random.normal(first, (CANDS, D), jnp.float32), -4.0, 4.0)
    return (base_rows * row_scale * col_scale).astype(jnp.bfloat16)


def place_ends(entries, key, smallest, largest):
    dims = entries.shape
    place = [jax.random.randint(jax.random.fold_in(key, axis), (), 0, dims[axis]) for axis in range(len(dims))]
    entries = entries.at[tuple(place)].set(smallest)
    longest = dims.index(max(dims))
    place[longest] = (place[longest] + 1) % dims[longest]
    return entries.at[tuple(place)].set(largest)


def block_scale(stream_key, extent, cuts, low, top_value):
    level, own = 1.0, jax.random.fold_in(stream_key, 6)
    for dim, shards_of in cuts:
        steps = jnp.exp(jax.random.uniform(jax.random.fold_in(own, dim), (shards_of,), jnp.float32, low / len(cuts), top_value / len(cuts)))
        level = level * jnp.repeat(steps, extent[dim] // shards_of).reshape([-1 if axis == dim else 1 for axis in range(len(extent))])
    return level


def length_profile(count, total, limit, slope):
    weights = [(1 << 20) // math.isqrt(standing ** slope) + 1 for standing in range(2, count + 1)]
    rest, given = total - limit - (count - 1), [1] * (count - 1)
    while rest > 0:
        free = [i for i in range(count - 1) if given[i] < limit]
        pool, left = sum([weights[i] for i in free]), rest
        for i in free:
            addition = min(limit - given[i], max(1, left * weights[i] // pool), rest)
            given[i] = given[i] + addition
            rest = rest - addition
    return np.array([limit] + given)


def ragged_sizes(own_key, count, total, limit, lean):
    if count == 2:
        one = jax.random.randint(own_key, (), max(1, total - limit), min(limit, total - 1) + 1)
        return jnp.stack([one, total - one])
    tallies = jnp.asarray(length_profile(count, total, limit, lean), jnp.int32)
    pairs = (count - 1) // 2
    donor, receiver = tallies[1:1 + 2 * pairs:2], tallies[2:2 + 2 * pairs:2]
    margin = jnp.minimum(donor - 1, limit - receiver)
    passed = jax.random.randint(jax.random.fold_in(own_key, 1), (pairs,), 0, 1 << 20) % (margin + 1)
    tallies = tallies.at[1:1 + 2 * pairs:2].set(donor - passed).at[2:2 + 2 * pairs:2].set(receiver + passed)
    return tallies[jax.random.permutation(jax.random.fold_in(own_key, 2), count)]


def deal_out(stream_key, own, number, rows, amount, top, most, lean):
    ranking = jax.random.permutation(stream_key, amount)
    heavy_load, usual = shares(amount, rows * top, most, lean, True), shares(amount, rows * top, most, lean, False)
    places = jnp.arange(amount)

    def named(sizes, turn):
        used = int((sizes > 0).sum())
        fixed = max(1, used // 4)
        moved = fixed + (places - fixed + turn * (used - fixed)) % max(1, amount - fixed)
        return jnp.zeros((amount,), jnp.int32).at[ranking[jnp.where(places < fixed, places, moved)]].set(jnp.asarray(sizes, jnp.int32))

    sizes = jnp.where(number % 4 == 0, named(heavy_load, number // 4), named(usual, number - number // 4 - 1))
    mixed = jax.random.permutation(jax.random.fold_in(own, 3), amount)
    source_of, sink = mixed[0:amount // 2 * 2:2], mixed[1:amount // 2 * 2:2]
    room = jnp.minimum(sizes[source_of] - 1, most - sizes[sink]) // 2
    room = jnp.where((source_of == ranking[0]) | (sink == ranking[0]) | (sizes[sink] == 0), 0, jnp.maximum(room, 0))
    moved = jax.random.randint(jax.random.fold_in(own, 4), (amount // 2,), 0, 1 << 20) % (room + 1)
    sizes = sizes.at[source_of].add(-moved).at[sink].add(moved)
    members = jnp.searchsorted(jnp.cumsum(sizes), jnp.arange(rows * top), side="right").astype(jnp.int32)
    grid = members.reshape(top, rows).T
    grid = grid[jax.random.permutation(jax.random.fold_in(own, 1), rows)]
    turn = jax.random.randint(jax.random.fold_in(own, 2), (rows, 1), 0, top)
    return jnp.take_along_axis(grid, (jnp.arange(top)[None, :] + turn) % top, axis=1)


def shares(number_of, total, limit, lean, full):
    portions = [(1 << 20) // math.isqrt(grade ** lean) + 1 for grade in range(1, number_of + 1)]
    largest = limit if full else min(limit, max(-(-total // number_of), total * portions[0] // sum(portions)))
    least = 1 if total - largest >= number_of - 1 else 0
    holding, rest = [largest] + [least] * (number_of - 1), total - largest - least * (number_of - 1)
    while rest > 0:
        free = [i for i in range(1, number_of) if holding[i] < largest] or [i for i in range(1, number_of) if holding[i] < limit]
        whole, remaining = sum([portions[i] for i in free]), rest
        for i in free:
            extra = min(limit - holding[i], max(1, remaining * portions[i] // whole), rest)
            holding[i] = holding[i] + extra
            rest = rest - extra
    return np.array(holding)


def normal_values(own_key, shape, deviation, most, cuts=(), kind=jnp.bfloat16):
    entries = jax.random.normal(own_key, shape, jnp.float32) * deviation
    if len(cuts) > 0:
        entries = block_scale(own_key, shape, cuts, -0.22, 0.18) * entries
    return jnp.clip(entries, min=-most, max=most).astype(kind)


def setup_inputs(seed: int = 0) -> dict:
    streams_of = jax.random.split(jax.random.key(seed), 9)
    cand_rows = draw_cand_rows(jax.random.fold_in(streams_of[8], 71), 0)
    proj_weight = normal_values(streams_of[1], (D, 4, HD), D ** -0.5, 0.1875, ((2, 8),))
    out_weight = normal_values(streams_of[2], (HD, D), (HD // 8) ** -0.5, 0.5, ((0, 8),))
    self_bias = jnp.clip(1.0 + 3.0 * jax.random.uniform(streams_of[3], (H,), jnp.float32) ** block_scale(streams_of[3], (H,), ((0, 8),), -0.2, 0.2), 1.0, 4.0)
    history_cache = normal_values(streams_of[4], (REQS, HMAX, 2, HD), 1.0, 6.0, ((0, 32), (3, 8)))
    history_length = ragged_sizes(streams_of[5], REQS, REQS * HMAX // 2, HMAX, 2).astype(jnp.int32)
    candidate_slot_keys = jax.random.split(jax.random.fold_in(streams_of[6], 1), CANDS // C_DEV)
    candidate_slot_turns = jax.random.permutation(jax.random.fold_in(streams_of[6], 3), CANDS // C_DEV)
    candidate_slot = jax.vmap(lambda own, number: deal_out(jax.random.fold_in(streams_of[6], 2), own, number, C_DEV, REQS, 1, CAPS, 1))(candidate_slot_keys, candidate_slot_turns).reshape((CANDS, 1))
    hot_slot = place_ends(jax.random.randint(streams_of[7], (N_SHARD,), 0, R_DEV), jax.random.fold_in(streams_of[7], 1), 0, R_DEV - 1).astype(jnp.int32)
    return dict(cand_rows=cand_rows, proj_weight=proj_weight, out_weight=out_weight, self_bias=self_bias, history_cache=history_cache, history_length=history_length, candidate_slot=candidate_slot, hot_slot=hot_slot)


epsilon = 1e-06

def attend_slot(query_rows, key_self, candidate_value, cache_slab, length, head_bias, head_count):
    score_scale = DH ** (-0.5)
    block_count = (length + KBLK - 1) // KBLK

    def add_block(block_index, running):
        offset = block_index * KBLK
        key_block = lax.dynamic_slice_in_dim(cache_slab, offset, KBLK, 0).astype(jnp.float32)
        history_key_rows = key_block[:, 0].reshape(KBLK, head_count, DH)
        history_value_rows = key_block[:, 1].reshape(KBLK, head_count, DH)
        scores = jnp.einsum('phd,khd->phk', query_rows, history_key_rows) * score_scale
        where_live = offset + jnp.arange(KBLK, dtype=jnp.int32) < length
        narrow = jnp.where(where_live[None, None, :], jax.nn.silu(scores), 0.0).astype(jnp.bfloat16)
        weight_matrices = lax.optimization_barrier(narrow).astype(jnp.float32)
        return running + jnp.einsum('phk,khd->phd', weight_matrices, history_value_rows)
    initial = jnp.zeros(query_rows.shape, jnp.float32)
    history = lax.fori_loop(0, block_count, add_block, initial)
    self_score = lax.optimization_barrier(jnp.sum(query_rows * key_self, axis=-1)) * score_scale + head_bias[None, :]
    merged = history + jax.nn.silu(self_score)[..., None] * candidate_value
    return merged.astype(jnp.bfloat16)

def reference(cand_rows, proj_weight, out_weight, self_bias, history_cache, history_length, candidate_slot, hot_slot):
    total_row_count = cand_rows.shape[0]
    head_width = H * DH
    wide_rows = cand_rows.astype(jnp.float32)
    mean_square = lax.optimization_barrier(jnp.mean(wide_rows * wide_rows, axis=1, keepdims=True))
    projected = jnp.dot(cand_rows, proj_weight.reshape(D, 4 * head_width), preferred_element_type=jnp.float32)
    projected = jax.nn.silu(projected / jnp.sqrt(mean_square + epsilon)).astype(jnp.bfloat16)
    projected = projected.reshape(total_row_count, 4, head_width)
    gate_rows = projected[:, 0]
    candidate_value = projected[:, 1]
    query_rows = projected[:, 2]
    own_keys = projected[:, 3]
    slot_ids = candidate_slot[:, 0]
    device_ids = slot_ids // R_DEV
    places = slot_ids % R_DEV
    half_axis = N_SHARD // 2
    partners = jnp.bitwise_xor(device_ids, half_axis)
    sources = jnp.where(places == hot_slot[device_ids], partners * R_DEV + hot_slot[partners], slot_ids).astype(jnp.int32)
    ordering = jnp.argsort(sources, stable=True).astype(jnp.int32)
    counts = jax.ops.segment_sum(jnp.ones_like(sources), sources, num_segments=REQS)
    starts = jnp.cumsum(counts) - counts
    padded = N_SHARD * CAPS

    def per_source(slot_index):
        lane_ids = jnp.arange(padded, dtype=jnp.int32)
        is_live = lane_ids < counts[slot_index]
        selected_rows = ordering[jnp.clip(starts[slot_index] + lane_ids, 0, total_row_count - 1)]
        q_rows = query_rows[selected_rows].astype(jnp.float32).reshape(padded, H, DH)
        k_rows = own_keys[selected_rows].astype(jnp.float32).reshape(padded, H, DH)
        v_rows = candidate_value[selected_rows].astype(jnp.float32).reshape(padded, H, DH)
        answer = attend_slot(q_rows, k_rows, v_rows, history_cache[slot_index], history_length[slot_index], self_bias.astype(jnp.float32), H)
        return (answer.reshape(padded, head_width), jnp.where(is_live, selected_rows, total_row_count).astype(jnp.int32))
    results, targets = lax.map(per_source, jnp.arange(REQS, dtype=jnp.int32))
    attention = jnp.zeros((total_row_count, head_width), jnp.bfloat16)
    attention = attention.at[targets.reshape(-1)].set(results.reshape(-1, head_width), mode='drop')
    attn_wide = attention.astype(jnp.float32).reshape(total_row_count, H, DH)
    normed = attn_wide / jnp.sqrt(lax.optimization_barrier(jnp.mean(attn_wide * attn_wide, axis=-1, keepdims=True)) + epsilon)
    hidden = (normed.reshape(total_row_count, head_width) * gate_rows.astype(jnp.float32)).astype(jnp.bfloat16)
    return (wide_rows + jnp.dot(hidden, out_weight, preferred_element_type=jnp.float32)).astype(jnp.bfloat16)
```

```python
import functools

import jax
import jax.numpy as jnp
from jax import lax
from jax.experimental import pallas as pl
from jax.experimental.pallas import tpu as pltpu
from jax.sharding import PartitionSpec as P

DH = 64
epsilon = 1e-06
BF = jnp.bfloat16
F32 = jnp.float32
ROWS = 256
SCATTER = 512
KBLK = 512
VMEM_LIMIT = 48 * 1024 * 1024


def dot(a, b):
    return jnp.dot(a, b, preferred_element_type=F32)


def inverse_rms(rows):
    wide = rows.astype(F32)
    return lax.rsqrt(jnp.mean(wide * wide, axis=1, keepdims=True) + epsilon)


def silu(x):
    half = 0.5 * x
    return half + half * jnp.tanh(half)


def query_kernel(capacity, cand_ref, weight_ref, slot_ref, source_ref, sent_ref, query_ref, key_ref, queries, keys, carry):
    step = pl.program_id(0)
    slot_total = source_ref.shape[0]
    column = source_ref[...].astype(F32) * capacity - 1.0

    @pl.when(step == 0)
    def _():
        carry[...] = jnp.zeros_like(carry)

    rows = cand_ref[...]
    query = silu(dot(rows, weight_ref[...]) * inverse_rms(rows)).astype(BF) * BF(0.5 * DH**-0.5)
    query_ref[...] = query
    start = pl.multiple_of(step * ROWS, ROWS)
    queries[pl.ds(start, ROWS), :] = query

    slots = slot_ref[:, pl.ds(start, ROWS)]
    member = (slots == lax.broadcasted_iota(jnp.int32, (slot_total, ROWS), 0)).astype(F32)
    before = lax.broadcasted_iota(jnp.int32, (ROWS, ROWS), 0) <= lax.broadcasted_iota(jnp.int32, (ROWS, ROWS), 1)
    counted = dot(member.astype(BF), before.astype(BF)) + carry[:, :1]
    carry[...] = jnp.broadcast_to(counted[:, ROWS - 1 :], carry.shape)
    keys[:, pl.ds(start, ROWS)] = jnp.sum(member * (counted + column), axis=0, keepdims=True).astype(jnp.int32)

    @pl.when(step == pl.num_programs(0) - 1)
    def _():
        key_ref[...] = keys[...]

        @pl.loop(0, slot_total * capacity // SCATTER)
        def _(block):
            per = SCATTER // capacity
            lane_keys = keys[...]
            local = lax.broadcasted_iota(jnp.int32, (capacity, lane_keys.shape[1]), 0)
            parts = [
                (lane_keys - (block * per + i) * capacity == local).astype(F32).astype(BF)
                for i in range(per)
            ]
            picked = dot(jnp.concatenate(parts, axis=0), queries[...])
            sent_ref[pl.ds(pl.multiple_of(block * SCATTER, SCATTER), SCATTER), :] = picked.astype(BF)


def side_kernel(cand_ref, weight_ref, query_ref, bias_ref, gate_ref, self_ref):
    rows = cand_ref[...]
    width = gate_ref.shape[1]
    parts = silu(dot(rows, weight_ref[...]) * inverse_rms(rows)).astype(BF)
    gate_ref[...] = parts[:, :width]
    value = parts[:, width : 2 * width].astype(F32)
    product = query_ref[...].astype(F32) * parts[:, 2 * width :].astype(F32)
    lane = lax.broadcasted_iota(jnp.int32, product.shape, 1)
    score = jnp.zeros_like(product)
    for head in range(width // DH):
        here = lane // DH == head
        total = jnp.sum(jnp.where(here, product, 0.0), axis=1, keepdims=True)
        score = jnp.where(here, 2.0 * total + bias_ref[head], score)
    self_ref[...] = silu(score) * value


def attend_kernel(length_ref, packet_ref, key_ref, value_ref, answer_ref, masked):
    shard_count, slot_count, item_count, width = packet_ref.shape
    heads = width // DH
    history = key_ref.shape[2]
    group = ROWS // item_count
    for slot in range(slot_count):
        length = length_ref[slot]
        blocks = (length + KBLK - 1) // KBLK
        lane = lax.broadcasted_iota(jnp.int32, (KBLK, width), 1)

        @pl.loop(0, blocks)
        def _(block):
            offset = pl.multiple_of(block * KBLK, KBLK)
            values = value_ref[slot, pl.ds(offset, KBLK), :]
            live = offset + lax.broadcasted_iota(jnp.int32, (KBLK, width), 0) < length
            for head in range(heads):
                masked[block, head * KBLK : (head + 1) * KBLK, :] = jnp.where(
                    live & (lane // DH == head), values.astype(F32), 0.0
                ).astype(BF)

        @pl.loop(0, shard_count // group)
        def _(part):
            rows = packet_ref[pl.ds(part * group, group), slot].reshape(ROWS, width)
            row_lane = lax.broadcasted_iota(jnp.int32, (ROWS, width), 1)
            stacked = jnp.concatenate(
                [jnp.where(row_lane // DH == head, rows.astype(F32), 0.0).astype(BF) for head in range(heads)], axis=0
            )

            def add_block(block, total):
                offset = pl.multiple_of(block * KBLK, KBLK)
                half = dot(stacked, key_ref[slot, :, pl.ds(offset, KBLK)])
                weights = (half + half * jnp.tanh(half)).astype(BF)
                wide = jnp.concatenate([weights[head * ROWS : (head + 1) * ROWS] for head in range(heads)], axis=1)
                return total + dot(wide, masked[block])

            total = lax.fori_loop(0, blocks, add_block, jnp.zeros((ROWS, width), F32))
            answer_ref[pl.ds(part * group, group), slot] = total.astype(BF).reshape(group, item_count, width)


def hidden_kernel(key_ref, returned_ref, self_ref, gate_ref, hidden_ref):
    rows, width = gate_ref.shape
    positions = returned_ref.shape[0]
    chosen = (key_ref[...] == lax.broadcasted_iota(jnp.int32, (rows, positions), 1)).astype(F32).astype(BF)
    attention = dot(chosen, returned_ref[...]) + self_ref[...]
    square = attention * attention
    high = square.astype(BF)
    low = (square - high.astype(F32)).astype(BF)
    same = (
        lax.broadcasted_iota(jnp.int32, (width, width), 0) // DH
        == lax.broadcasted_iota(jnp.int32, (width, width), 1) // DH
    )
    ones = same.astype(F32).astype(BF)
    mean = (dot(high, ones) + dot(low, ones)) * (1.0 / DH)
    hidden_ref[...] = (attention * lax.rsqrt(mean + epsilon) * gate_ref[...].astype(F32)).astype(BF)


def output_kernel(place_ref, hidden_ref, weight_ref, residual_ref, out_ref):
    hidden = jnp.concatenate([hidden_ref[i] for i in range(hidden_ref.shape[0])], axis=1)
    mixed = (residual_ref[...].astype(F32) + dot(hidden, weight_ref[...])).astype(BF)
    part = out_ref.shape[2]
    for i in range(out_ref.shape[0]):
        out_ref[i] = mixed[:, i * part : (i + 1) * part]


def params(**more):
    return pltpu.CompilerParams(vmem_limit_bytes=VMEM_LIMIT, **more)


def body(cand_rows, proj_weight, out_weight, self_bias, history_cache, history_length, candidate_slot, hot_slot):
    shard_count = lax.axis_size("shard")
    my_shard = lax.axis_index("shard")
    tensor_count = lax.axis_size("tensor")
    my_tensor = lax.axis_index("tensor")
    row_count, model_width = cand_rows.shape
    width = out_weight.shape[0]
    slot_count = history_cache.shape[0]
    slot_total = shard_count * slot_count
    capacity = 2 * row_count // slot_total
    history = history_cache.shape[1]
    positions = slot_total * capacity
    steps = row_count // ROWS

    shards = jnp.arange(shard_count, dtype=jnp.int32)
    others = shards ^ (shard_count // 2)
    partner_hot = jnp.concatenate([hot_slot[shard_count // 2 :], hot_slot[: shard_count // 2]])
    local = jnp.arange(slot_count, dtype=jnp.int32)
    named = shards[:, None] * slot_count + local[None, :]
    sources = jnp.where(
        local[None, :] == hot_slot[:, None], (others * slot_count + partner_hot)[:, None], named
    ).reshape(slot_total, 1)

    full_weight = lax.all_gather(out_weight, "tensor", axis=0, tiled=True)

    query_weight = proj_weight[:, 2, :]
    slot_row = candidate_slot.reshape(1, row_count)
    sent, queries, keys = pl.pallas_call(
        functools.partial(query_kernel, capacity),
        grid=(steps,),
        in_specs=[
            pl.BlockSpec((ROWS, model_width), lambda i: (i, 0)),
            pl.BlockSpec((model_width, width), lambda i: (0, 0)),
            pl.BlockSpec((1, row_count), lambda i: (0, 0)),
            pl.BlockSpec((slot_total, 1), lambda i: (0, 0)),
        ],
        out_specs=[
            pl.BlockSpec((positions, width), lambda i: (0, 0)),
            pl.BlockSpec((ROWS, width), lambda i: (i, 0)),
            pl.BlockSpec((1, row_count), lambda i: (0, 0)),
        ],
        out_shape=[
            jax.ShapeDtypeStruct((positions, width), BF),
            jax.ShapeDtypeStruct((row_count, width), BF),
            jax.ShapeDtypeStruct((1, row_count), jnp.int32),
        ],
        scratch_shapes=[
            pltpu.VMEM((row_count, width), BF),
            pltpu.VMEM((1, row_count), jnp.int32),
            pltpu.VMEM((slot_total, 128), F32),
        ],
        compiler_params=params(),
        cost_estimate=pl.CostEstimate(flops=4 * 10**9, bytes_accessed=6 * 2**20, transcendentals=2**18),
        name="query",
    )(cand_rows, query_weight, slot_row, sources)

    received = lax.all_to_all(
        sent.reshape(shard_count, slot_count * capacity, width), "shard", split_axis=0, concat_axis=0, tiled=True
    ).reshape(shard_count, slot_count, capacity, width)

    side_weight = jnp.concatenate([proj_weight[:, 0], proj_weight[:, 1], proj_weight[:, 3]], axis=1)
    gate, self_term = pl.pallas_call(
        side_kernel,
        grid=(steps,),
        in_specs=[
            pl.BlockSpec((ROWS, model_width), lambda i: (i, 0)),
            pl.BlockSpec((model_width, 3 * width), lambda i: (0, 0)),
            pl.BlockSpec((ROWS, width), lambda i: (i, 0)),
            pl.BlockSpec(memory_space=pltpu.SMEM),
        ],
        out_specs=[pl.BlockSpec((ROWS, width), lambda i: (i, 0)), pl.BlockSpec((ROWS, width), lambda i: (i, 0))],
        out_shape=[jax.ShapeDtypeStruct((row_count, width), BF), jax.ShapeDtypeStruct((row_count, width), F32)],
        compiler_params=params(),
        cost_estimate=pl.CostEstimate(flops=4 * 10**9, bytes_accessed=6 * 2**20, transcendentals=2**20),
        name="side",
    )(cand_rows, side_weight, queries, self_bias)

    cache_keys = jnp.swapaxes(history_cache[:, :, 0, :], 1, 2)
    cache_values = history_cache[:, :, 1, :]
    key_column = keys.reshape(row_count, 1)
    lengths = lax.dynamic_slice_in_dim(history_length, my_shard * slot_count, slot_count)

    answered = pl.pallas_call(
        attend_kernel,
        in_specs=[pl.BlockSpec(memory_space=pltpu.SMEM)] + [pl.BlockSpec(memory_space=pltpu.VMEM)] * 3,
        out_specs=pl.BlockSpec(memory_space=pltpu.VMEM),
        out_shape=jax.ShapeDtypeStruct(received.shape, BF),
        scratch_shapes=[pltpu.VMEM((history // KBLK, width // DH * KBLK, width), BF)],
        compiler_params=params(),
        cost_estimate=pl.CostEstimate(flops=12 * 10**9, bytes_accessed=4 * 2**20, transcendentals=2**24),
        name="attend",
    )(lengths, received, cache_keys, cache_values)

    returned = lax.all_to_all(
        answered.reshape(shard_count, slot_count * capacity, width), "shard", split_axis=0, concat_axis=0, tiled=True
    ).reshape(positions, width)

    hidden_rows = 512
    hidden = pl.pallas_call(
        hidden_kernel,
        grid=(row_count // hidden_rows,),
        in_specs=[
            pl.BlockSpec((hidden_rows, 1), lambda i: (i, 0)),
            pl.BlockSpec((positions, width), lambda i: (0, 0)),
            pl.BlockSpec((hidden_rows, width), lambda i: (i, 0)),
            pl.BlockSpec((hidden_rows, width), lambda i: (i, 0)),
        ],
        out_specs=pl.BlockSpec((hidden_rows, width), lambda i: (i, 0)),
        out_shape=jax.ShapeDtypeStruct((row_count, width), BF),
        compiler_params=params(),
        cost_estimate=pl.CostEstimate(flops=4 * 10**9, bytes_accessed=4 * 2**20, transcendentals=2**18),
        name="hidden",
    )(key_column, returned, self_term, gate)

    owned = row_count // tensor_count
    gathered = lax.all_to_all(
        hidden.reshape(tensor_count, owned, width), "tensor", split_axis=0, concat_axis=0, tiled=True
    )
    out_width = model_width // tensor_count
    mixed = pl.pallas_call(
        output_kernel,
        grid_spec=pltpu.PrefetchScalarGridSpec(
            num_scalar_prefetch=1,
            grid=(tensor_count // 2,),
            in_specs=[
                pl.BlockSpec((tensor_count, owned, width), lambda i, place: (0, 0, 0)),
                pl.BlockSpec((model_width, 2 * out_width), lambda i, place: (0, i)),
                pl.BlockSpec((owned, 2 * out_width), lambda i, place: (place[0], i)),
            ],
            out_specs=pl.BlockSpec((2, owned, out_width), lambda i, place: (i, 0, 0)),
        ),
        out_shape=jax.ShapeDtypeStruct((tensor_count, owned, out_width), BF),
        compiler_params=params(),
        cost_estimate=pl.CostEstimate(flops=10**9, bytes_accessed=4 * 2**20, transcendentals=0),
        name="output",
    )(my_tensor.reshape(1).astype(jnp.int32), gathered, full_weight, cand_rows)
    placed = lax.all_to_all(mixed, "tensor", split_axis=0, concat_axis=0, tiled=True)
    return placed.reshape(row_count, out_width)


def solution(mesh):
    in_specs = (
        P("shard", None),
        P(None, None, "tensor"),
        P("tensor", None),
        P("tensor"),
        P("shard", None, None, "tensor"),
        P(),
        P("shard", None),
        P(),
    )
    out_specs = P("shard", "tensor")
    return jax.shard_map(body, mesh=mesh, in_specs=in_specs, out_specs=out_specs, check_vma=False)
```

```python
import functools

import jax
import jax.numpy as jnp
from jax import lax
from jax.experimental import pallas as pl
from jax.experimental.pallas import tpu as pltpu
from jax.sharding import PartitionSpec as P

DH = 64
epsilon = 1e-06
BF = jnp.bfloat16
F32 = jnp.float32
I32 = jnp.int32
PARTS = 4
QUERY = 2
CHUNK = 512
RANKED = 256
ROWS = 256
TILE = 16
KBLK = 512
BATCH = 32
MARK = 2.0**20
MIB = 1024 * 1024


def dot(a, b):
    return jnp.dot(a, b, preferred_element_type=F32)


def inverse_rms(rows):
    wide = rows.astype(F32)
    return lax.rsqrt(jnp.mean(wide * wide, axis=1, keepdims=True) + epsilon)


def silu(x):
    half = 0.5 * x
    return half + half * jnp.tanh(half)


def query_kernel(
    capacity, slot_count, cand_ref, weight_ref, slot_ref, hot_ref, sent_ref, query_ref, place_ref,
    rows, raw, wide, weight, places, queries, sent, packed, row_sem, raw_sem, place_sem, out_sem,
):
    row_count, model_width = rows.shape
    shard_count = hot_ref.shape[1]
    slot_total = shard_count * slot_count
    chunks = row_count // CHUNK
    raw_copy = pltpu.make_async_copy(weight_ref, raw, raw_sem)
    raw_copy.start()
    row_copies = []
    for i in range(chunks):
        part = pl.ds(i * CHUNK, CHUNK)
        row_copies.append(pltpu.make_async_copy(cand_ref.at[part], rows.at[part], row_sem.at[i]))
        row_copies[i].start()

    before = lax.broadcasted_iota(I32, (RANKED, RANKED), 0) <= lax.broadcasted_iota(I32, (RANKED, RANKED), 1)
    before = before.astype(F32).astype(BF)
    slots = lax.broadcasted_iota(I32, (8, slot_total), 1)
    other = (slots // slot_count) ^ (shard_count // 2)
    hot = jnp.broadcast_to(hot_ref[...].astype(F32), (8, shard_count)).astype(BF)
    shard = lax.broadcasted_iota(I32, (shard_count, slot_total), 0)
    owner = lax.broadcasted_iota(I32, (shard_count, slot_total), 1) // slot_count
    own_hot = dot(hot, (shard == owner).astype(F32).astype(BF)).astype(I32)
    other_hot = dot(hot, (shard == owner ^ (shard_count // 2)).astype(F32).astype(BF)).astype(I32)
    source = jnp.where(slots % slot_count == own_hot, other * slot_count + other_hot, slots).astype(F32).astype(BF)
    carry = jnp.zeros((slot_total, 1), F32)
    for i in range(row_count // RANKED):
        part = slice(i * RANKED, (i + 1) * RANKED)
        member = (slot_ref[:, part] == lax.broadcasted_iota(I32, (slot_total, RANKED), 0)).astype(F32)
        narrow = member.astype(BF)
        counted = dot(narrow, before) + carry
        carry = counted[:, RANKED - 1 :]
        base = dot(source, narrow)[:1]
        rank = jnp.sum(member * counted, axis=0, keepdims=True) - 1.0
        place_ref[:, part] = (base * capacity + rank).astype(I32)
    place_copy = pltpu.make_async_copy(place_ref, places, place_sem)
    place_copy.start()

    sent[...] = jnp.full(sent.shape, MARK, F32)
    raw_copy.wait()
    wide[...] = raw[...].astype(F32)
    weight[...] = wide[pl.ds(QUERY, model_width, stride=PARTS), :].astype(BF)
    for i in range(chunks):
        part = pl.ds(i * CHUNK, CHUNK)
        row_copies[i].wait()
        block = rows[part, :]
        query = silu(dot(block, weight[...]) * inverse_rms(block)).astype(BF) * BF(0.5 * DH**-0.5)
        query_ref[part, :] = query
        queries[part, :] = query.astype(F32)
    place_copy.wait()

    @pl.loop(0, row_count // BATCH)
    def _(i):
        start = pl.multiple_of(i * BATCH, BATCH)
        for j in range(BATCH):
            sent[pl.ds(places[0, start + j], 1), :] = queries[pl.ds(start + j, 1), :]

    out_copies = []
    quarter = sent.shape[0] // 4
    for i in range(4):
        part = pl.ds(i * quarter, quarter)
        packed[part, :] = sent[part, :].astype(BF)
        out_copies.append(pltpu.make_async_copy(packed.at[part], sent_ref.at[part], out_sem.at[i]))
        out_copies[i].start()
    for copy in out_copies:
        copy.wait()


def side_kernel(cand_ref, weight_ref, query_ref, bias_ref, gate_ref, self_ref, wide, weight):
    width = gate_ref.shape[1]
    model_width = cand_ref.shape[1]

    @pl.when(pl.program_id(0) == 0)
    def _():
        wide[...] = weight_ref[...].astype(F32)
        for i, part in enumerate((0, 1, 3)):
            weight[:, i * width : (i + 1) * width] = wide[pl.ds(part, model_width, stride=PARTS), :].astype(BF)

    rows = cand_ref[...]
    parts = silu(dot(rows, weight[...]) * inverse_rms(rows)).astype(BF)
    gate_ref[...] = parts[:, :width]
    value = parts[:, width : 2 * width].astype(F32)
    product = query_ref[...].astype(F32) * parts[:, 2 * width :].astype(F32)
    lane = lax.broadcasted_iota(I32, product.shape, 1)
    score = jnp.zeros_like(product)
    for head in range(width // DH):
        here = lane // DH == head
        total = jnp.sum(jnp.where(here, product, 0.0), axis=1, keepdims=True)
        score = jnp.where(here, 2.0 * total + bias_ref[head], score)
    self_ref[...] = silu(score) * value


def history_kernel(length_ref, cache_ref, keys_ref, values_ref, wide):
    slot_count, width, total = keys_ref.shape
    heads = width // DH
    history = total // heads
    value_lane = lax.broadcasted_iota(I32, (KBLK, width), 1)
    key_row = lax.broadcasted_iota(I32, (width, KBLK), 0)
    for slot in range(slot_count):
        length = length_ref[slot]
        wide[...] = cache_ref[slot].astype(F32)
        for block in range(history // KBLK):
            keys = wide[pl.ds(2 * block * KBLK, KBLK, stride=2), :].T
            values = wide[pl.ds(2 * block * KBLK + 1, KBLK, stride=2), :]
            live = block * KBLK + lax.broadcasted_iota(I32, (KBLK, width), 0) < length
            for head in range(heads):
                start = (block * heads + head) * KBLK
                place = slice(start, start + KBLK)
                values_ref[slot, place, :] = jnp.where(live & (value_lane // DH == head), values, 0.0).astype(BF)
                keys_ref[slot, :, place] = jnp.where(key_row // DH == head, keys, 0.0).astype(BF)


def attend_kernel(
    length_ref, packet_ref, keys_hbm, values_hbm, answer_ref,
    keys_ref, values_ref, packed, totals, answers, flag_rows, flags, flag_sem, in_sem, out_sem,
):
    shard_count, slot_count, item_count, width = packet_ref.shape
    heads = width // DH
    per = item_count // TILE
    together = 4
    history = values_ref.shape[1] // heads
    ones = jnp.ones((8, width), BF)
    in_copies = []
    for slot in range(slot_count):
        in_copies.append(pltpu.make_async_copy(keys_hbm.at[slot], keys_ref.at[slot], in_sem.at[2 * slot]))
        in_copies.append(pltpu.make_async_copy(values_hbm.at[slot], values_ref.at[slot], in_sem.at[2 * slot + 1]))
    for copy in in_copies:
        copy.start()
    for slot in range(slot_count):
        rows = packet_ref[:, slot].reshape(shard_count * item_count, width)
        sums = lax.dot_general(ones, rows, (((1,), (1,)), ((), ())), preferred_element_type=F32)
        flag_rows[slot : slot + 1, :] = jnp.where(sums[:1] < MARK, TILE, 0).astype(I32)
    flag_copy = pltpu.make_async_copy(flag_rows, flags, flag_sem)
    flag_copy.start()
    flag_copy.wait()
    out_copies = []
    for slot in range(slot_count):
        blocks = (length_ref[slot] + KBLK - 1) // KBLK

        def pack(i, offset):
            tiles = [
                packet_ref[i * together + j, slot, k * TILE : (k + 1) * TILE, :]
                for j in range(together)
                for k in range(per)
            ]
            for j, tile in enumerate(tiles):
                packed[pl.ds(pl.multiple_of(offset, TILE), TILE), :] = tile
                offset = offset + flags[slot, (i * together * per + j) * TILE]
            return offset

        total_rows = lax.fori_loop(0, shard_count // together, pack, jnp.int32(0))
        row_blocks = (total_rows + ROWS - 1) // ROWS
        in_copies[2 * slot].wait()
        in_copies[2 * slot + 1].wait()

        for k in range(1, history // KBLK + 1):

            @pl.when(blocks == k)
            def _():
                @pl.loop(0, row_blocks)
                def _(part):
                    start = pl.multiple_of(part * ROWS, ROWS)
                    rows = packed[pl.ds(start, ROWS), :]

                    def score(j):
                        return dot(rows, keys_ref[slot, :, j * KBLK : (j + 1) * KBLK])

                    total = jnp.zeros((ROWS, width), F32)
                    half = score(0)
                    for j in range(heads * k):
                        later = score(j + 1) if j + 1 < heads * k else None
                        weights = (half + half * jnp.tanh(half)).astype(BF)
                        total = total + dot(weights, values_ref[slot, j * KBLK : (j + 1) * KBLK, :])
                        half = later
                    totals[pl.ds(start, ROWS), :] = total.astype(BF)

        def unpack(i, offset):
            tiles = []
            for j in range(together * per):
                tiles.append(totals[pl.ds(pl.multiple_of(offset, TILE), TILE), :])
                offset = offset + flags[slot, (i * together * per + j) * TILE]
            for j in range(together):
                for k in range(per):
                    answers[slot, i * together + j, k * TILE : (k + 1) * TILE, :] = tiles[j * per + k]
            return offset

        lax.fori_loop(0, shard_count // together, unpack, jnp.int32(0))
        out_copies.append(pltpu.make_async_copy(answers.at[slot], answer_ref.at[:, slot], out_sem.at[slot]))
        out_copies[slot].start()
    for copy in out_copies:
        copy.wait()


def hidden_kernel(place_ref, returned_ref, self_hbm, gate_hbm, hidden_ref, self_ref, gate_ref, wide, chosen, in_sem):
    row_count, width = chosen.shape
    self_copy = pltpu.make_async_copy(self_hbm, self_ref, in_sem.at[0])
    gate_copy = pltpu.make_async_copy(gate_hbm, gate_ref, in_sem.at[1])
    self_copy.start()
    gate_copy.start()
    wide[...] = returned_ref[...].astype(F32)

    @pl.loop(0, row_count // BATCH)
    def _(i):
        start = pl.multiple_of(i * BATCH, BATCH)
        for j in range(BATCH):
            chosen[pl.ds(start + j, 1), :] = wide[pl.ds(place_ref[start + j], 1), :]

    self_copy.wait()
    gate_copy.wait()
    same = lax.broadcasted_iota(I32, (width, width), 0) // DH == lax.broadcasted_iota(I32, (width, width), 1) // DH
    ones = same.astype(F32).astype(BF)
    for i in range(row_count // CHUNK):
        part = pl.ds(i * CHUNK, CHUNK)
        attention = chosen[part, :] + self_ref[part, :]
        square = attention * attention
        high = square.astype(BF)
        low = (square - high.astype(F32)).astype(BF)
        mean = (dot(high, ones) + dot(low, ones)) * (1.0 / DH)
        hidden_ref[part, :] = (attention * lax.rsqrt(mean + epsilon) * gate_ref[part, :].astype(F32)).astype(BF)


def output_kernel(
    place_ref, hidden_ref, own_hbm, other_hbm, residual_hbm, out_ref, weight, residual, weight_sem, residual_sem
):
    count, owned, width = hidden_ref.shape
    place = place_ref[0]
    core = place_ref[1]
    copies = []
    for step in range(count):
        source = place ^ sum((count >> (bit + 1)) for bit in range(3) if step >> bit & 1)
        part = pl.ds(pl.multiple_of(source * width, width), width)
        for half, ref in ((core, own_hbm), (1 - core, other_hbm)):
            copies.append(pltpu.make_async_copy(ref.at[step], weight.at[half, part], weight_sem.at[len(copies)]))
    rows = pl.ds(pl.multiple_of(place * owned, owned), owned)
    copies.append(pltpu.make_async_copy(residual_hbm.at[rows], residual, residual_sem))
    for copy in copies:
        copy.start()
    hidden = jnp.concatenate([hidden_ref[i] for i in range(count)], axis=1)
    for copy in copies:
        copy.wait()
    part = out_ref.shape[2]
    for i in range(0, count, 2):
        half, first = divmod(i, count // 2)
        columns = slice(first * part, (first + 2) * part)
        wide = residual[:, i * part : (i + 2) * part].astype(F32)
        mixed = (wide + dot(hidden, weight[half, :, columns])).astype(BF)
        out_ref[i] = mixed[:, :part]
        out_ref[i + 1] = mixed[:, part:]


def params(limit):
    return pltpu.CompilerParams(vmem_limit_bytes=limit * MIB)


ANY = pl.BlockSpec(memory_space=pl.ANY)
WHOLE = pl.BlockSpec(memory_space=pltpu.VMEM)
SCALARS = pl.BlockSpec(memory_space=pltpu.SMEM)


def body(cand_rows, proj_weight, out_weight, self_bias, history_cache, history_length, candidate_slot, hot_slot):
    shard_count = lax.axis_size("shard")
    my_shard = lax.axis_index("shard")
    tensor_count = lax.axis_size("tensor")
    my_tensor = lax.axis_index("tensor")
    row_count, model_width = cand_rows.shape
    width = out_weight.shape[0]
    heads = width // DH
    slot_count = history_cache.shape[0]
    slot_total = shard_count * slot_count
    capacity = 2 * row_count // slot_total
    history = history_cache.shape[1]
    positions = slot_total * capacity
    dma = pltpu.SemaphoreType.DMA

    core = my_shard % 2
    half_width = model_width // 2
    weight_half = lax.dynamic_slice_in_dim(out_weight, core * half_width, half_width, 1)[None]

    def swap(array, axis, distance):
        return lax.ppermute(array, axis, [(i, i ^ distance) for i in range(lax.axis_size(axis))])

    def double(array, distance):
        return jnp.concatenate([array, swap(array, "tensor", distance)], axis=0)

    weights = proj_weight.reshape(model_width * PARTS, width)
    slot_row = candidate_slot.reshape(1, row_count)
    sent, queries, places = pl.pallas_call(
        functools.partial(query_kernel, capacity, slot_count),
        in_specs=[ANY, ANY, WHOLE, WHOLE],
        out_specs=[ANY, WHOLE, WHOLE],
        out_shape=[
            jax.ShapeDtypeStruct((positions, width), BF),
            jax.ShapeDtypeStruct((row_count, width), BF),
            jax.ShapeDtypeStruct((1, row_count), I32),
        ],
        scratch_shapes=[
            pltpu.VMEM((row_count, model_width), BF),
            pltpu.VMEM((model_width * PARTS, width), BF),
            pltpu.VMEM((model_width * PARTS, width), F32),
            pltpu.VMEM((model_width, width), BF),
            pltpu.SMEM((1, row_count), I32),
            pltpu.VMEM((row_count, width), F32),
            pltpu.VMEM((positions, width), F32),
            pltpu.VMEM((positions, width), BF),
            dma((row_count // CHUNK,)),
            dma,
            dma,
            dma((4,)),
        ],
        compiler_params=params(60),
        cost_estimate=pl.CostEstimate(flops=4 * 10**9, bytes_accessed=6 * 2**20, transcendentals=2**18),
        name="query",
    )(cand_rows, weights, slot_row, hot_slot.reshape(1, shard_count))

    received = lax.all_to_all(
        sent.reshape(shard_count, slot_count * capacity, width), "shard", split_axis=0, concat_axis=0, tiled=True
    ).reshape(shard_count, slot_count, capacity, width)

    block = 512
    gate, self_term = pl.pallas_call(
        side_kernel,
        grid=(row_count // block,),
        in_specs=[
            pl.BlockSpec((block, model_width), lambda i: (i, 0)),
            pl.BlockSpec((model_width * PARTS, width), lambda i: (0, 0)),
            pl.BlockSpec((block, width), lambda i: (i, 0)),
            SCALARS,
        ],
        out_specs=[pl.BlockSpec((block, width), lambda i: (i, 0)), pl.BlockSpec((block, width), lambda i: (i, 0))],
        out_shape=[jax.ShapeDtypeStruct((row_count, width), BF), jax.ShapeDtypeStruct((row_count, width), F32)],
        scratch_shapes=[
            pltpu.VMEM((model_width * PARTS, width), F32),
            pltpu.VMEM((model_width, (PARTS - 1) * width), BF),
        ],
        compiler_params=params(32),
        cost_estimate=pl.CostEstimate(flops=4 * 10**9, bytes_accessed=6 * 2**20, transcendentals=2**20),
        name="side",
    )(cand_rows, weights, queries, self_bias)

    lengths = lax.dynamic_slice_in_dim(history_length, my_shard * slot_count, slot_count)
    head_keys, head_values = pl.pallas_call(
        history_kernel,
        grid=(1,),
        in_specs=[SCALARS, pl.BlockSpec((slot_count, 2 * history, width), lambda i: (0, 0, 0))],
        out_specs=[
            pl.BlockSpec((slot_count, width, heads * history), lambda i: (0, 0, 0)),
            pl.BlockSpec((slot_count, heads * history, width), lambda i: (0, 0, 0)),
        ],
        out_shape=[
            jax.ShapeDtypeStruct((slot_count, width, heads * history), BF),
            jax.ShapeDtypeStruct((slot_count, heads * history, width), BF),
        ],
        scratch_shapes=[pltpu.VMEM((2 * history, width), F32)],
        compiler_params=params(56),
        cost_estimate=pl.CostEstimate(flops=10**9, bytes_accessed=6 * 2**20, transcendentals=0),
        name="history",
    )(lengths, history_cache.reshape(slot_count, 2 * history, width))

    weight_two = double(weight_half, tensor_count // 2)
    received, weight_two, gate, self_term, head_keys, head_values = lax.optimization_barrier(
        (received, weight_two, gate, self_term, head_keys, head_values)
    )
    weight_four = double(weight_two, tensor_count // 4)
    answered = pl.pallas_call(
        attend_kernel,
        in_specs=[SCALARS, WHOLE, ANY, ANY],
        out_specs=ANY,
        out_shape=jax.ShapeDtypeStruct(received.shape, BF),
        scratch_shapes=[
            pltpu.VMEM(head_keys.shape, BF),
            pltpu.VMEM(head_values.shape, BF),
            pltpu.VMEM((shard_count * capacity + ROWS, width), BF),
            pltpu.VMEM((shard_count * capacity + ROWS, width), BF),
            pltpu.VMEM((slot_count, shard_count, capacity, width), BF),
            pltpu.VMEM((slot_count, shard_count * capacity), I32),
            pltpu.SMEM((slot_count, shard_count * capacity), I32),
            dma,
            dma((2 * slot_count,)),
            dma((slot_count,)),
        ],
        compiler_params=params(48),
        cost_estimate=pl.CostEstimate(flops=12 * 10**9, bytes_accessed=4 * 2**20, transcendentals=2**24),
        name="attend",
    )(lengths, received, head_keys, head_values)

    answered, weight_four = lax.optimization_barrier((answered, weight_four))
    weight_all = double(weight_four, tensor_count // 8)
    returned = lax.all_to_all(
        answered.reshape(shard_count, slot_count * capacity, width), "shard", split_axis=0, concat_axis=0, tiled=True
    ).reshape(positions, width)

    returned, weight_all = lax.optimization_barrier((returned, weight_all))
    other_half = swap(weight_all, "shard", 1)
    hidden = pl.pallas_call(
        hidden_kernel,
        in_specs=[SCALARS, WHOLE, ANY, ANY],
        out_specs=WHOLE,
        out_shape=jax.ShapeDtypeStruct((row_count, width), BF),
        scratch_shapes=[
            pltpu.VMEM((row_count, width), F32),
            pltpu.VMEM((row_count, width), BF),
            pltpu.VMEM((positions, width), F32),
            pltpu.VMEM((row_count, width), F32),
            dma((2,)),
        ],
        compiler_params=params(40),
        cost_estimate=pl.CostEstimate(flops=4 * 10**9, bytes_accessed=4 * 2**20, transcendentals=2**18),
        name="hidden",
    )(places.reshape(row_count), returned, self_term, gate)

    place = my_tensor.reshape(1).astype(I32)
    place = jnp.concatenate([place, core.reshape(1).astype(I32)])
    hidden, weight_all, other_half, place = lax.optimization_barrier((hidden, weight_all, other_half, place))
    owned = row_count // tensor_count
    gathered = lax.all_to_all(
        hidden.reshape(tensor_count, owned, width), "tensor", split_axis=0, concat_axis=0, tiled=True
    )
    out_width = model_width // tensor_count
    mixed = pl.pallas_call(
        output_kernel,
        in_specs=[SCALARS, WHOLE, ANY, ANY, ANY],
        out_specs=WHOLE,
        out_shape=jax.ShapeDtypeStruct((tensor_count, owned, out_width), BF),
        scratch_shapes=[
            pltpu.VMEM((2, model_width, half_width), BF),
            pltpu.VMEM((owned, model_width), BF),
            dma((2 * tensor_count,)),
            dma,
        ],
        compiler_params=params(58),
        cost_estimate=pl.CostEstimate(flops=10**9, bytes_accessed=4 * 2**20, transcendentals=0),
        name="output",
    )(place, gathered, weight_all, other_half, cand_rows)
    placed = lax.all_to_all(mixed, "tensor", split_axis=0, concat_axis=0, tiled=True)
    return placed.reshape(row_count, out_width)


def solution(mesh):
    in_specs = (
        P("shard", None),
        P(None, None, "tensor"),
        P("tensor", None),
        P("tensor"),
        P("shard", None, None, "tensor"),
        P(),
        P("shard", None),
        P(),
    )
    out_specs = P("shard", "tensor")
    return jax.shard_map(body, mesh=mesh, in_specs=in_specs, out_specs=out_specs, check_vma=False)
```

```python
import functools

import jax
import jax.numpy as jnp
from jax import lax
from jax.experimental import pallas as pl
from jax.experimental.pallas import tpu as pltpu
from jax.sharding import PartitionSpec as P

DH = 64
epsilon = 1e-06
BF = jnp.bfloat16
F32 = jnp.float32
I32 = jnp.int32
PARTS = 4
QUERY = 2
CHUNK = 512
RANKED = 256
ROWS = 256
TILE = 16
KBLK = 512
BATCH = 32
MARK = 2.0**20
MIB = 1024 * 1024


def dot(a, b):
    return jnp.dot(a, b, preferred_element_type=F32)


def inverse_rms(rows):
    wide = rows.astype(F32)
    return lax.rsqrt(jnp.mean(wide * wide, axis=1, keepdims=True) + epsilon)


def silu(x):
    half = 0.5 * x
    return half + half * jnp.tanh(half)


def query_kernel(
    capacity, slot_count, cand_ref, weight_ref, slot_ref, hot_ref, sent_ref, query_ref, place_ref,
    rows, raw, wide, weight, places, queries, sent, packed, row_sem, raw_sem, place_sem, out_sem,
):
    row_count, model_width = rows.shape
    shard_count = hot_ref.shape[1]
    slot_total = shard_count * slot_count
    chunks = row_count // CHUNK
    raw_copy = pltpu.make_async_copy(weight_ref, raw, raw_sem)
    raw_copy.start()
    row_copies = []
    for i in range(chunks):
        part = pl.ds(i * CHUNK, CHUNK)
        row_copies.append(pltpu.make_async_copy(cand_ref.at[part], rows.at[part], row_sem.at[i]))
        row_copies[i].start()

    before = lax.broadcasted_iota(I32, (RANKED, RANKED), 0) <= lax.broadcasted_iota(I32, (RANKED, RANKED), 1)
    before = before.astype(F32).astype(BF)
    slots = lax.broadcasted_iota(I32, (8, slot_total), 1)
    other = (slots // slot_count) ^ (shard_count // 2)
    hot = jnp.broadcast_to(hot_ref[...].astype(F32), (8, shard_count)).astype(BF)
    shard = lax.broadcasted_iota(I32, (shard_count, slot_total), 0)
    owner = lax.broadcasted_iota(I32, (shard_count, slot_total), 1) // slot_count
    own_hot = dot(hot, (shard == owner).astype(F32).astype(BF)).astype(I32)
    other_hot = dot(hot, (shard == owner ^ (shard_count // 2)).astype(F32).astype(BF)).astype(I32)
    source = jnp.where(slots % slot_count == own_hot, other * slot_count + other_hot, slots).astype(F32).astype(BF)
    carry = jnp.zeros((slot_total, 1), F32)
    for i in range(row_count // RANKED):
        part = slice(i * RANKED, (i + 1) * RANKED)
        member = (slot_ref[:, part] == lax.broadcasted_iota(I32, (slot_total, RANKED), 0)).astype(F32)
        narrow = member.astype(BF)
        counted = dot(narrow, before) + carry
        carry = counted[:, RANKED - 1 :]
        base = dot(source, narrow)[:1]
        rank = jnp.sum(member * counted, axis=0, keepdims=True) - 1.0
        place_ref[:, part] = (base * capacity + rank).astype(I32)
    place_copy = pltpu.make_async_copy(place_ref, places, place_sem)
    place_copy.start()

    sent[...] = jnp.full(sent.shape, MARK, F32)
    raw_copy.wait()
    wide[...] = raw[...].astype(F32)
    weight[...] = wide[pl.ds(QUERY, model_width, stride=PARTS), :].astype(BF)
    for i in range(chunks):
        part = pl.ds(i * CHUNK, CHUNK)
        row_copies[i].wait()
        block = rows[part, :]
        query = silu(dot(block, weight[...]) * inverse_rms(block)).astype(BF) * BF(0.5 * DH**-0.5)
        query_ref[part, :] = query
        queries[part, :] = query.astype(F32)
    place_copy.wait()

    @pl.loop(0, row_count // BATCH)
    def _(i):
        start = pl.multiple_of(i * BATCH, BATCH)
        for j in range(BATCH):
            sent[pl.ds(places[0, start + j], 1), :] = queries[pl.ds(start + j, 1), :]

    out_copies = []
    quarter = sent.shape[0] // 4
    for i in range(4):
        part = pl.ds(i * quarter, quarter)
        packed[part, :] = sent[part, :].astype(BF)
        out_copies.append(pltpu.make_async_copy(packed.at[part], sent_ref.at[part], out_sem.at[i]))
        out_copies[i].start()
    for copy in out_copies:
        copy.wait()


def side_kernel(cand_ref, weight_ref, query_ref, bias_ref, pair_ref, wide, weight):
    width = pair_ref.shape[1] // 2
    model_width = cand_ref.shape[1]

    @pl.when(pl.program_id(0) == 0)
    def _():
        wide[...] = weight_ref[...].astype(F32)
        for i, part in enumerate((0, 1, 3)):
            weight[:, i * width : (i + 1) * width] = wide[pl.ds(part, model_width, stride=PARTS), :].astype(BF)

    rows = cand_ref[...]
    parts = silu(dot(rows, weight[...]) * inverse_rms(rows)).astype(BF)
    pair_ref[:, :width] = parts[:, :width].astype(F32)
    value = parts[:, width : 2 * width].astype(F32)
    product = query_ref[...].astype(F32) * parts[:, 2 * width :].astype(F32)
    lane = lax.broadcasted_iota(I32, product.shape, 1)
    score = jnp.zeros_like(product)
    for head in range(width // DH):
        here = lane // DH == head
        total = jnp.sum(jnp.where(here, product, 0.0), axis=1, keepdims=True)
        score = jnp.where(here, 2.0 * total + bias_ref[head], score)
    pair_ref[:, width:] = silu(score) * value


def history_kernel(length_ref, cache_ref, keys_ref, values_ref, wide):
    slot_count, width, total = keys_ref.shape
    heads = width // DH
    history = total // heads
    value_lane = lax.broadcasted_iota(I32, (KBLK, width), 1)
    key_row = lax.broadcasted_iota(I32, (width, KBLK), 0)
    for slot in range(slot_count):
        length = length_ref[slot]
        wide[...] = cache_ref[slot].astype(F32)
        for block in range(history // KBLK):
            keys = wide[pl.ds(2 * block * KBLK, KBLK, stride=2), :].T
            values = wide[pl.ds(2 * block * KBLK + 1, KBLK, stride=2), :]
            live = block * KBLK + lax.broadcasted_iota(I32, (KBLK, width), 0) < length
            for head in range(heads):
                start = (block * heads + head) * KBLK
                place = slice(start, start + KBLK)
                values_ref[slot, place, :] = jnp.where(live & (value_lane // DH == head), values, 0.0).astype(BF)
                keys_ref[slot, :, place] = jnp.where(key_row // DH == head, keys, 0.0).astype(BF)


def attend_kernel(
    length_ref, packet_ref, keys_hbm, values_hbm, answer_ref,
    keys_ref, values_ref, packed, totals, answers, flag_rows, flags, flag_sem, in_sem, out_sem,
):
    shard_count, slot_count, item_count, width = packet_ref.shape
    heads = width // DH
    per = item_count // TILE
    together = 4
    history = values_ref.shape[1] // heads
    ones = jnp.ones((8, width), BF)
    in_copies = []
    for slot in range(slot_count):
        in_copies.append(pltpu.make_async_copy(keys_hbm.at[slot], keys_ref.at[slot], in_sem.at[2 * slot]))
        in_copies.append(pltpu.make_async_copy(values_hbm.at[slot], values_ref.at[slot], in_sem.at[2 * slot + 1]))
    for copy in in_copies:
        copy.start()
    for slot in range(slot_count):
        rows = packet_ref[:, slot].reshape(shard_count * item_count, width)
        sums = lax.dot_general(ones, rows, (((1,), (1,)), ((), ())), preferred_element_type=F32)
        flag_rows[slot : slot + 1, :] = jnp.where(sums[:1] < MARK, TILE, 0).astype(I32)
    flag_copy = pltpu.make_async_copy(flag_rows, flags, flag_sem)
    flag_copy.start()
    flag_copy.wait()
    out_copies = []
    for slot in range(slot_count):
        blocks = (length_ref[slot] + KBLK - 1) // KBLK

        def pack(i, offset):
            tiles = [
                packet_ref[i * together + j, slot, k * TILE : (k + 1) * TILE, :]
                for j in range(together)
                for k in range(per)
            ]
            for j, tile in enumerate(tiles):
                packed[pl.ds(pl.multiple_of(offset, TILE), TILE), :] = tile
                offset = offset + flags[slot, (i * together * per + j) * TILE]
            return offset

        total_rows = lax.fori_loop(0, shard_count // together, pack, jnp.int32(0))
        row_blocks = (total_rows + ROWS - 1) // ROWS
        in_copies[2 * slot].wait()
        in_copies[2 * slot + 1].wait()

        for k in range(1, history // KBLK + 1):

            @pl.when(blocks == k)
            def _():
                @pl.loop(0, row_blocks)
                def _(part):
                    start = pl.multiple_of(part * ROWS, ROWS)
                    rows = packed[pl.ds(start, ROWS), :]

                    def score(j):
                        return dot(rows, keys_ref[slot, :, j * KBLK : (j + 1) * KBLK])

                    total = jnp.zeros((ROWS, width), F32)
                    half = score(0)
                    for j in range(heads * k):
                        later = score(j + 1) if j + 1 < heads * k else None
                        weights = (half + half * jnp.tanh(half)).astype(BF)
                        total = total + dot(weights, values_ref[slot, j * KBLK : (j + 1) * KBLK, :])
                        half = later
                    totals[pl.ds(start, ROWS), :] = total.astype(BF)

        def unpack(i, offset):
            tiles = []
            for j in range(together * per):
                tiles.append(totals[pl.ds(pl.multiple_of(offset, TILE), TILE), :])
                offset = offset + flags[slot, (i * together * per + j) * TILE]
            for j in range(together):
                for k in range(per):
                    answers[slot, i * together + j, k * TILE : (k + 1) * TILE, :] = tiles[j * per + k]
            return offset

        lax.fori_loop(0, shard_count // together, unpack, jnp.int32(0))
        out_copies.append(pltpu.make_async_copy(answers.at[slot], answer_ref.at[:, slot], out_sem.at[slot]))
        out_copies[slot].start()
    for copy in out_copies:
        copy.wait()


def hidden_kernel(place_ref, returned_ref, pair_hbm, hidden_ref, pair_ref, wide, chosen, pair_sem):
    row_count, width = chosen.shape
    pair_copy = pltpu.make_async_copy(pair_hbm, pair_ref, pair_sem)
    pair_copy.start()
    wide[...] = returned_ref[...].astype(F32)

    @pl.loop(0, row_count // BATCH)
    def _(i):
        start = pl.multiple_of(i * BATCH, BATCH)
        for j in range(BATCH):
            chosen[pl.ds(start + j, 1), :] = wide[pl.ds(place_ref[start + j], 1), :]

    pair_copy.wait()
    same = lax.broadcasted_iota(I32, (width, width), 0) // DH == lax.broadcasted_iota(I32, (width, width), 1) // DH
    ones = same.astype(F32).astype(BF)
    for i in range(row_count // CHUNK):
        part = pl.ds(i * CHUNK, CHUNK)
        attention = chosen[part, :] + pair_ref[part, width:]
        square = attention * attention
        high = square.astype(BF)
        low = (square - high.astype(F32)).astype(BF)
        mean = (dot(high, ones) + dot(low, ones)) * (1.0 / DH)
        hidden_ref[part, :] = (attention * lax.rsqrt(mean + epsilon) * pair_ref[part, :width]).astype(BF)


def output_kernel(
    place_ref, hidden_ref, own_four, own_five, other_four, other_five, residual_ref, out_ref
):
    count, owned, width = hidden_ref.shape
    place = lax.div(place_ref[0], 2)
    core = lax.rem(place_ref[0], 2)
    order = [flip ^ i for i in range(2) for flip in (0, 4, 2, 6)]
    hidden = jnp.concatenate([hidden_ref[place ^ flip] for flip in order], axis=1)
    part = out_ref.shape[2]
    half_width = own_four.shape[2]
    products = []
    for half, refs in ((core, (own_four, own_five)), (1 - core, (other_four, other_five))):
        blocks = [ref[...].reshape(-1, half_width) for ref in refs]
        products.append((half, dot(hidden, jnp.concatenate(blocks, axis=0))))
    for half, product in products:
        start = pl.multiple_of(half * half_width, half_width)
        mixed = (residual_ref[:, pl.ds(start, half_width)].astype(F32) + product).astype(BF)
        for i in range(half_width // part):
            out_ref[half * (half_width // part) + i] = mixed[:, i * part : (i + 1) * part]


def params(limit):
    return pltpu.CompilerParams(vmem_limit_bytes=limit * MIB)


ANY = pl.BlockSpec(memory_space=pl.ANY)
WHOLE = pl.BlockSpec(memory_space=pltpu.VMEM)
SCALARS = pl.BlockSpec(memory_space=pltpu.SMEM)


def body(cand_rows, proj_weight, out_weight, self_bias, history_cache, history_length, candidate_slot, hot_slot):
    shard_count = lax.axis_size("shard")
    my_shard = lax.axis_index("shard")
    tensor_count = lax.axis_size("tensor")
    my_tensor = lax.axis_index("tensor")
    row_count, model_width = cand_rows.shape
    width = out_weight.shape[0]
    heads = width // DH
    slot_count = history_cache.shape[0]
    slot_total = shard_count * slot_count
    capacity = 2 * row_count // slot_total
    history = history_cache.shape[1]
    positions = slot_total * capacity
    dma = pltpu.SemaphoreType.DMA

    core = my_shard % 2
    half_width = model_width // 2
    weight_half = lax.dynamic_slice_in_dim(out_weight, core * half_width, half_width, 1)[None]

    def swap(array, axis, distance):
        return lax.ppermute(array, axis, [(i, i ^ distance) for i in range(lax.axis_size(axis))])

    weights = proj_weight.reshape(model_width * PARTS, width)
    slot_row = candidate_slot.reshape(1, row_count)
    sent, queries, places = pl.pallas_call(
        functools.partial(query_kernel, capacity, slot_count),
        in_specs=[ANY, ANY, WHOLE, WHOLE],
        out_specs=[ANY, WHOLE, WHOLE],
        out_shape=[
            jax.ShapeDtypeStruct((positions, width), BF),
            jax.ShapeDtypeStruct((row_count, width), BF),
            jax.ShapeDtypeStruct((1, row_count), I32),
        ],
        scratch_shapes=[
            pltpu.VMEM((row_count, model_width), BF),
            pltpu.VMEM((model_width * PARTS, width), BF),
            pltpu.VMEM((model_width * PARTS, width), F32),
            pltpu.VMEM((model_width, width), BF),
            pltpu.SMEM((1, row_count), I32),
            pltpu.VMEM((row_count, width), F32),
            pltpu.VMEM((positions, width), F32),
            pltpu.VMEM((positions, width), BF),
            dma((row_count // CHUNK,)),
            dma,
            dma,
            dma((4,)),
        ],
        compiler_params=params(60),
        cost_estimate=pl.CostEstimate(flops=4 * 10**9, bytes_accessed=6 * 2**20, transcendentals=2**18),
        name="query",
    )(cand_rows, weights, slot_row, hot_slot.reshape(1, shard_count))

    sent, weight_half = lax.optimization_barrier((sent, weight_half))
    weight_one = swap(weight_half, "tensor", tensor_count // 2)
    received = lax.all_to_all(
        sent.reshape(shard_count, slot_count * capacity, width), "shard", split_axis=0, concat_axis=0, tiled=True
    ).reshape(shard_count, slot_count, capacity, width)

    lengths = lax.dynamic_slice_in_dim(history_length, my_shard * slot_count, slot_count)
    head_keys, head_values = pl.pallas_call(
        history_kernel,
        grid=(1,),
        in_specs=[SCALARS, pl.BlockSpec((slot_count, 2 * history, width), lambda i: (0, 0, 0))],
        out_specs=[
            pl.BlockSpec((slot_count, width, heads * history), lambda i: (0, 0, 0)),
            pl.BlockSpec((slot_count, heads * history, width), lambda i: (0, 0, 0)),
        ],
        out_shape=[
            jax.ShapeDtypeStruct((slot_count, width, heads * history), BF),
            jax.ShapeDtypeStruct((slot_count, heads * history, width), BF),
        ],
        scratch_shapes=[pltpu.VMEM((2 * history, width), F32)],
        compiler_params=params(60),
        cost_estimate=pl.CostEstimate(flops=10**9, bytes_accessed=6 * 2**20, transcendentals=0),
        name="history",
    )(lengths, history_cache.reshape(slot_count, 2 * history, width))

    weight_two = jnp.concatenate([weight_half, weight_one], axis=0)
    weight_three = swap(weight_two, "tensor", tensor_count // 4)
    answered = pl.pallas_call(
        attend_kernel,
        in_specs=[SCALARS, WHOLE, ANY, ANY],
        out_specs=ANY,
        out_shape=jax.ShapeDtypeStruct(received.shape, BF),
        scratch_shapes=[
            pltpu.VMEM(head_keys.shape, BF),
            pltpu.VMEM(head_values.shape, BF),
            pltpu.VMEM((shard_count * capacity + ROWS, width), BF),
            pltpu.VMEM((shard_count * capacity + ROWS, width), BF),
            pltpu.VMEM((slot_count, shard_count, capacity, width), BF),
            pltpu.VMEM((slot_count, shard_count * capacity), I32),
            pltpu.SMEM((slot_count, shard_count * capacity), I32),
            dma,
            dma((2 * slot_count,)),
            dma((slot_count,)),
        ],
        compiler_params=params(61),
        cost_estimate=pl.CostEstimate(flops=12 * 10**9, bytes_accessed=4 * 2**20, transcendentals=2**24),
        name="attend",
    )(lengths, received, head_keys, head_values)

    answered, weight_three, queries = lax.optimization_barrier((answered, weight_three, queries))
    weight_four = jnp.concatenate([weight_two, weight_three], axis=0)
    weight_five = swap(weight_four, "tensor", tensor_count // 8)
    returned = lax.all_to_all(
        answered.reshape(shard_count, slot_count * capacity, width), "shard", split_axis=0, concat_axis=0, tiled=True
    ).reshape(positions, width)

    returned, weight_five = lax.optimization_barrier((returned, weight_five))
    other_four = swap(weight_four, "shard", 1)
    other_five = swap(weight_five, "shard", 1)
    block = 512
    gate_and_self = pl.pallas_call(
        side_kernel,
        grid=(row_count // block,),
        in_specs=[
            pl.BlockSpec((block, model_width), lambda i: (i, 0)),
            pl.BlockSpec((model_width * PARTS, width), lambda i: (0, 0)),
            pl.BlockSpec((block, width), lambda i: (i, 0)),
            SCALARS,
        ],
        out_specs=pl.BlockSpec((block, 2 * width), lambda i: (i, 0)),
        out_shape=jax.ShapeDtypeStruct((row_count, 2 * width), F32),
        scratch_shapes=[
            pltpu.VMEM((model_width * PARTS, width), F32),
            pltpu.VMEM((model_width, (PARTS - 1) * width), BF),
        ],
        compiler_params=params(32),
        cost_estimate=pl.CostEstimate(flops=4 * 10**9, bytes_accessed=6 * 2**20, transcendentals=2**20),
        name="side",
    )(cand_rows, weights, queries, self_bias)

    owned = row_count // tensor_count
    place = (2 * my_tensor + core).reshape(1).astype(I32)
    residual = lax.dynamic_slice_in_dim(cand_rows, my_tensor * owned, owned, 0)

    hidden = pl.pallas_call(
        hidden_kernel,
        in_specs=[SCALARS, WHOLE, ANY],
        out_specs=WHOLE,
        out_shape=jax.ShapeDtypeStruct((row_count, width), BF),
        scratch_shapes=[
            pltpu.VMEM((row_count, 2 * width), F32),
            pltpu.VMEM((positions, width), F32),
            pltpu.VMEM((row_count, width), F32),
            dma,
        ],
        compiler_params=params(61),
        cost_estimate=pl.CostEstimate(flops=4 * 10**9, bytes_accessed=4 * 2**20, transcendentals=2**18),
        name="hidden",
    )(places.reshape(row_count), returned, gate_and_self)

    gathered = lax.all_to_all(
        hidden.reshape(tensor_count, owned, width), "tensor", split_axis=0, concat_axis=0, tiled=True
    )
    out_width = model_width // tensor_count
    mixed = pl.pallas_call(
        output_kernel,
        in_specs=[SCALARS] + [WHOLE] * 6,
        out_specs=WHOLE,
        out_shape=jax.ShapeDtypeStruct((tensor_count, owned, out_width), BF),
        compiler_params=params(24),
        cost_estimate=pl.CostEstimate(flops=10**9, bytes_accessed=4 * 2**20, transcendentals=0),
        name="output",
    )(place, gathered, weight_four, weight_five, other_four, other_five, residual)
    placed = lax.all_to_all(mixed, "tensor", split_axis=0, concat_axis=0, tiled=True)
    return placed.reshape(row_count, out_width)


def solution(mesh):
    in_specs = (
        P("shard", None),
        P(None, None, "tensor"),
        P("tensor", None),
        P("tensor"),
        P("shard", None, None, "tensor"),
        P(),
        P("shard", None),
        P(),
    )
    out_specs = P("shard", "tensor")
    return jax.shard_map(body, mesh=mesh, in_specs=in_specs, out_specs=out_specs, check_vma=False)
```

```python
import functools

import jax
import jax.numpy as jnp
from jax import lax
from jax.experimental import pallas as pl
from jax.experimental.pallas import tpu as pltpu
from jax.sharding import PartitionSpec as P

DH = 64
epsilon = 1e-06
BF = jnp.bfloat16
F32 = jnp.float32
I32 = jnp.int32
PARTS = 4
QUERY = 2
CHUNK = 1024
NORMED = 512
RANKED = 256
ROWS = 256
TILE = 16
KBLK = 512
BATCH = 64
MARK = 2.0**20
MIB = 1024 * 1024


def dot(a, b):
    return jnp.dot(a, b, preferred_element_type=F32)


def inverse_rms(rows):
    wide = rows.astype(F32)
    return lax.rsqrt(jnp.mean(wide * wide, axis=1, keepdims=True) + epsilon)


def silu(x):
    half = 0.5 * x
    return half + half * jnp.tanh(half)


def query_kernel(
    capacity, slot_count, cand_ref, weight_ref, slot_ref, hot_ref, sent_ref, query_ref, place_ref,
    rows, raw, wide, weight, places, queries, sent, packed, row_sem, raw_sem, place_sem, out_sem,
):
    row_count, model_width = rows.shape
    shard_count = hot_ref.shape[1]
    slot_total = shard_count * slot_count
    chunks = row_count // CHUNK
    raw_copy = pltpu.make_async_copy(weight_ref, raw, raw_sem)
    raw_copy.start()
    row_copies = []
    for i in range(chunks):
        part = pl.ds(i * CHUNK, CHUNK)
        row_copies.append(pltpu.make_async_copy(cand_ref.at[part], rows.at[part], row_sem.at[i]))
        row_copies[i].start()

    before = lax.broadcasted_iota(I32, (RANKED, RANKED), 0) <= lax.broadcasted_iota(I32, (RANKED, RANKED), 1)
    before = before.astype(F32).astype(BF)
    slots = lax.broadcasted_iota(I32, (8, slot_total), 1)
    other = (slots // slot_count) ^ (shard_count // 2)
    hot = jnp.broadcast_to(hot_ref[...].astype(F32), (8, shard_count)).astype(BF)
    shard = lax.broadcasted_iota(I32, (shard_count, slot_total), 0)
    owner = lax.broadcasted_iota(I32, (shard_count, slot_total), 1) // slot_count
    own_hot = dot(hot, (shard == owner).astype(F32).astype(BF)).astype(I32)
    other_hot = dot(hot, (shard == owner ^ (shard_count // 2)).astype(F32).astype(BF)).astype(I32)
    source = jnp.where(slots % slot_count == own_hot, other * slot_count + other_hot, slots).astype(F32).astype(BF)
    carry = jnp.zeros((slot_total, 1), F32)
    for i in range(row_count // RANKED):
        part = slice(i * RANKED, (i + 1) * RANKED)
        member = (slot_ref[:, part] == lax.broadcasted_iota(I32, (slot_total, RANKED), 0)).astype(F32)
        narrow = member.astype(BF)
        counted = dot(narrow, before) + carry
        carry = counted[:, RANKED - 1 :]
        base = dot(source, narrow)[:1]
        rank = jnp.sum(member * counted, axis=0, keepdims=True) - 1.0
        place_ref[:, part] = (base * capacity + rank).astype(I32)
    place_copy = pltpu.make_async_copy(place_ref, places, place_sem)
    place_copy.start()

    sent[...] = jnp.full(sent.shape, MARK, F32)
    raw_copy.wait()
    wide[...] = raw[...].astype(F32)
    weight[...] = wide[pl.ds(QUERY, model_width, stride=PARTS), :].astype(BF)
    for i in range(chunks):
        part = pl.ds(i * CHUNK, CHUNK)
        row_copies[i].wait()
        block = rows[part, :]
        query = silu(dot(block, weight[...]) * inverse_rms(block)).astype(BF) * BF(0.5 * DH**-0.5)
        query_ref[part, :] = query
        queries[part, :] = query.astype(F32)
    place_copy.wait()

    @pl.loop(0, row_count // BATCH)
    def _(i):
        start = pl.multiple_of(i * BATCH, BATCH)
        for j in range(BATCH):
            sent[pl.ds(places[0, start + j], 1), :] = queries[pl.ds(start + j, 1), :]

    out_copies = []
    quarter = sent.shape[0] // 4
    for i in range(4):
        part = pl.ds(i * quarter, quarter)
        packed[part, :] = sent[part, :].astype(BF)
        out_copies.append(pltpu.make_async_copy(packed.at[part], sent_ref.at[part], out_sem.at[i]))
        out_copies[i].start()
    for copy in out_copies:
        copy.wait()


def side_kernel(cand_ref, weight_ref, query_ref, bias_ref, pair_ref, wide, weight):
    width = pair_ref.shape[1] // 2
    model_width = cand_ref.shape[1]

    @pl.when(pl.program_id(0) == 0)
    def _():
        wide[...] = weight_ref[...].astype(F32)
        for i, part in enumerate((0, 1, 3)):
            weight[:, i * width : (i + 1) * width] = wide[pl.ds(part, model_width, stride=PARTS), :].astype(BF)

    rows = cand_ref[...]
    parts = silu(dot(rows, weight[...]) * inverse_rms(rows)).astype(BF)
    pair_ref[:, :width] = parts[:, :width].astype(F32)
    value = parts[:, width : 2 * width].astype(F32)
    product = query_ref[...].astype(F32) * parts[:, 2 * width :].astype(F32)
    lane = lax.broadcasted_iota(I32, product.shape, 1)
    score = jnp.zeros_like(product)
    for head in range(width // DH):
        here = lane // DH == head
        total = jnp.sum(jnp.where(here, product, 0.0), axis=1, keepdims=True)
        score = jnp.where(here, 2.0 * total + bias_ref[head], score)
    pair_ref[:, width:] = silu(score) * value


def history_kernel(length_ref, cache_ref, out_ref, wide):
    slot_count, total, width = cache_ref.shape
    heads = width // DH
    history = total // 2
    value_lane = lax.broadcasted_iota(I32, (KBLK, width), 1)
    key_row = lax.broadcasted_iota(I32, (width, KBLK), 0)
    for slot in range(slot_count):
        length = length_ref[slot]
        wide[...] = cache_ref[slot].astype(F32)
        for block in range(history // KBLK):
            keys = wide[pl.ds(2 * block * KBLK, KBLK, stride=2), :].T
            values = wide[pl.ds(2 * block * KBLK + 1, KBLK, stride=2), :]
            live = block * KBLK + lax.broadcasted_iota(I32, (KBLK, width), 0) < length
            for head in range(heads):
                start = (block * heads + head) * KBLK
                out_ref[slot, 0, start : start + KBLK, :] = jnp.where(
                    live & (value_lane // DH == head), values, 0.0
                ).astype(BF)
                part = jnp.where(key_row // DH == head, keys, 0.0).astype(BF)
                for i in range(KBLK // width):
                    place = slice(start + i * width, start + (i + 1) * width)
                    out_ref[slot, 1, place, :] = part[:, i * width : (i + 1) * width]


def attend_kernel(
    length_ref, packet_ref, cache_hbm, answer_ref,
    cache_ref, packed, totals, answers, flag_rows, flags, flag_sem, in_sem, out_sem,
):
    shard_count, slot_count, item_count, width = packet_ref.shape
    heads = width // DH
    per = item_count // TILE
    together = 4
    history = cache_ref.shape[2] // heads
    ones = jnp.ones((8, width), BF)
    in_copies = []
    for slot in range(slot_count):
        in_copies.append(pltpu.make_async_copy(cache_hbm.at[slot], cache_ref.at[slot], in_sem.at[slot]))
    for copy in in_copies:
        copy.start()
    for slot in range(slot_count):
        rows = packet_ref[:, slot].reshape(shard_count * item_count, width)
        sums = lax.dot_general(ones, rows, (((1,), (1,)), ((), ())), preferred_element_type=F32)
        flag_rows[slot : slot + 1, :] = jnp.where(sums[:1] < MARK, TILE, 0).astype(I32)
    flag_copy = pltpu.make_async_copy(flag_rows, flags, flag_sem)
    flag_copy.start()
    flag_copy.wait()
    out_copies = []
    for slot in range(slot_count):
        blocks = (length_ref[slot] + KBLK - 1) // KBLK

        def pack(i, offset):
            tiles = [
                packet_ref[i * together + j, slot, k * TILE : (k + 1) * TILE, :]
                for j in range(together)
                for k in range(per)
            ]
            for j, tile in enumerate(tiles):
                packed[pl.ds(pl.multiple_of(offset, TILE), TILE), :] = tile
                offset = offset + flags[slot, (i * together * per + j) * TILE]
            return offset

        total_rows = lax.fori_loop(0, shard_count // together, pack, jnp.int32(0))
        row_blocks = (total_rows + ROWS // 2 - 1) // ROWS
        in_copies[slot].wait()

        def attend_rows(start, count, blocks_here):
            rows = packed[pl.ds(start, count), :]

            def score(j):
                parts = [
                    cache_ref[slot, 1, j * KBLK + i * width : j * KBLK + (i + 1) * width, :]
                    for i in range(KBLK // width)
                ]
                return dot(rows, jnp.concatenate(parts, axis=1))

            total = jnp.zeros((count, width), F32)
            half = score(0)
            for j in range(heads * blocks_here):
                later = score(j + 1) if j + 1 < heads * blocks_here else None
                weights = (half + half * jnp.tanh(half)).astype(BF)
                total = total + dot(weights, cache_ref[slot, 0, j * KBLK : (j + 1) * KBLK, :])
                half = later
            totals[pl.ds(start, count), :] = total.astype(BF)

        for k in range(1, history // KBLK + 1):

            @pl.when(blocks == k)
            def _():
                @pl.loop(0, row_blocks)
                def _(part):
                    attend_rows(pl.multiple_of(part * ROWS, ROWS), ROWS, k)

                @pl.when(total_rows > row_blocks * ROWS)
                def _():
                    attend_rows(pl.multiple_of(row_blocks * ROWS, ROWS), ROWS // 2, k)

        def unpack(i, offset):
            tiles = []
            for j in range(together * per):
                tiles.append(totals[pl.ds(pl.multiple_of(offset, TILE), TILE), :])
                offset = offset + flags[slot, (i * together * per + j) * TILE]
            for j in range(together):
                for k in range(per):
                    answers[slot, i * together + j, k * TILE : (k + 1) * TILE, :] = tiles[j * per + k]
            return offset

        lax.fori_loop(0, shard_count // together, unpack, jnp.int32(0))
        out_copies.append(pltpu.make_async_copy(answers.at[slot], answer_ref.at[:, slot], out_sem.at[slot]))
        out_copies[slot].start()
    for copy in out_copies:
        copy.wait()


def hidden_kernel(place_ref, returned_ref, pair_hbm, hidden_ref, pair_ref, wide, chosen, pair_sem):
    row_count, width = chosen.shape
    pair_copy = pltpu.make_async_copy(pair_hbm, pair_ref, pair_sem)
    pair_copy.start()
    wide[...] = returned_ref[...].astype(F32)

    @pl.loop(0, row_count // BATCH)
    def _(i):
        start = pl.multiple_of(i * BATCH, BATCH)
        for j in range(BATCH):
            chosen[pl.ds(start + j, 1), :] = wide[pl.ds(place_ref[start + j], 1), :]

    pair_copy.wait()
    same = lax.broadcasted_iota(I32, (width, width), 0) // DH == lax.broadcasted_iota(I32, (width, width), 1) // DH
    ones = same.astype(F32).astype(BF)
    for i in range(row_count // NORMED):
        part = pl.ds(i * NORMED, NORMED)
        attention = chosen[part, :] + pair_ref[part, width:]
        square = attention * attention
        high = square.astype(BF)
        low = (square - high.astype(F32)).astype(BF)
        mean = (dot(high, ones) + dot(low, ones)) * (1.0 / DH)
        hidden_ref[part, :] = (attention * lax.rsqrt(mean + epsilon) * pair_ref[part, :width]).astype(BF)


def output_kernel(
    place_ref, hidden_ref, residual_ref, own_0, own_1, own_2, own_3, other_0, other_1, other_2, other_3, out_ref
):
    count, owned, width = hidden_ref.shape
    place = lax.div(place_ref[0], 2)
    core = lax.rem(place_ref[0], 2)
    order = [flip ^ i for i in range(2) for flip in (0, 4, 2, 6)]
    hidden = jnp.concatenate([hidden_ref[place ^ flip] for flip in order], axis=1)
    part = out_ref.shape[2]
    half_width = own_0.shape[2]
    products = []
    for half, refs in ((core, (own_0, own_1, own_2, own_3)), (1 - core, (other_0, other_1, other_2, other_3))):
        product = residual_ref[:, pl.ds(pl.multiple_of(half * half_width, half_width), half_width)].astype(F32)
        for i, ref in enumerate(refs):
            deep = hidden.shape[1] // len(refs)
            product = product + dot(hidden[:, i * deep : (i + 1) * deep], ref[...].reshape(deep, half_width))
        products.append((half, product))
    for half, product in products:
        mixed = product.astype(BF)
        for i in range(half_width // part):
            out_ref[half * (half_width // part) + i] = mixed[:, i * part : (i + 1) * part]


def params(limit):
    return pltpu.CompilerParams(vmem_limit_bytes=limit * MIB)


ANY = pl.BlockSpec(memory_space=pl.ANY)
WHOLE = pl.BlockSpec(memory_space=pltpu.VMEM)
SCALARS = pl.BlockSpec(memory_space=pltpu.SMEM)


def body(cand_rows, proj_weight, out_weight, self_bias, history_cache, history_length, candidate_slot, hot_slot):
    shard_count = lax.axis_size("shard")
    my_shard = lax.axis_index("shard")
    tensor_count = lax.axis_size("tensor")
    my_tensor = lax.axis_index("tensor")
    row_count, model_width = cand_rows.shape
    width = out_weight.shape[0]
    heads = width // DH
    slot_count = history_cache.shape[0]
    slot_total = shard_count * slot_count
    capacity = 2 * row_count // slot_total
    history = history_cache.shape[1]
    positions = slot_total * capacity
    dma = pltpu.SemaphoreType.DMA

    core = my_shard % 2
    half_width = model_width // 2
    weight_half = lax.dynamic_slice_in_dim(out_weight, core * half_width, half_width, 1)[None]

    def swap(array, axis, distance):
        return lax.ppermute(array, axis, [(i, i ^ distance) for i in range(lax.axis_size(axis))])

    weights = proj_weight.reshape(model_width * PARTS, width)
    slot_row = candidate_slot.reshape(1, row_count)
    sent, queries, places = pl.pallas_call(
        functools.partial(query_kernel, capacity, slot_count),
        in_specs=[ANY, ANY, WHOLE, WHOLE],
        out_specs=[ANY, WHOLE, WHOLE],
        out_shape=[
            jax.ShapeDtypeStruct((positions, width), BF),
            jax.ShapeDtypeStruct((row_count, width), BF),
            jax.ShapeDtypeStruct((1, row_count), I32),
        ],
        scratch_shapes=[
            pltpu.VMEM((row_count, model_width), BF),
            pltpu.VMEM((model_width * PARTS, width), BF),
            pltpu.VMEM((model_width * PARTS, width), F32),
            pltpu.VMEM((model_width, width), BF),
            pltpu.SMEM((1, row_count), I32),
            pltpu.VMEM((row_count, width), F32),
            pltpu.VMEM((positions, width), F32),
            pltpu.VMEM((positions, width), BF),
            dma((row_count // CHUNK,)),
            dma,
            dma,
            dma((4,)),
        ],
        compiler_params=params(60),
        cost_estimate=pl.CostEstimate(flops=4 * 10**9, bytes_accessed=6 * 2**20, transcendentals=2**18),
        name="query",
    )(cand_rows, weights, slot_row, hot_slot.reshape(1, shard_count))

    sent, weight_half = lax.optimization_barrier((sent, weight_half))
    weight_one = swap(weight_half, "tensor", tensor_count // 2)
    received = lax.all_to_all(
        sent.reshape(shard_count, slot_count * capacity, width), "shard", split_axis=0, concat_axis=0, tiled=True
    ).reshape(shard_count, slot_count, capacity, width)

    lengths = lax.dynamic_slice_in_dim(history_length, my_shard * slot_count, slot_count)
    head_cache = pl.pallas_call(
        history_kernel,
        grid=(1,),
        in_specs=[SCALARS, pl.BlockSpec((slot_count, 2 * history, width), lambda i: (0, 0, 0))],
        out_specs=pl.BlockSpec((slot_count, 2, heads * history, width), lambda i: (0, 0, 0, 0)),
        out_shape=jax.ShapeDtypeStruct((slot_count, 2, heads * history, width), BF),
        scratch_shapes=[pltpu.VMEM((2 * history, width), F32)],
        compiler_params=params(60),
        cost_estimate=pl.CostEstimate(flops=10**9, bytes_accessed=6 * 2**20, transcendentals=0),
        name="history",
    )(lengths, history_cache.reshape(slot_count, 2 * history, width))

    weight_two = jnp.concatenate([weight_half, weight_one], axis=0)
    weight_three = swap(weight_two, "tensor", tensor_count // 4)
    weight_four = swap(weight_two, "tensor", tensor_count // 8)
    answered = pl.pallas_call(
        attend_kernel,
        in_specs=[SCALARS, WHOLE, ANY],
        out_specs=ANY,
        out_shape=jax.ShapeDtypeStruct(received.shape, BF),
        scratch_shapes=[
            pltpu.VMEM(head_cache.shape, BF),
            pltpu.VMEM((shard_count * capacity + ROWS, width), BF),
            pltpu.VMEM((shard_count * capacity + ROWS, width), BF),
            pltpu.VMEM((slot_count, shard_count, capacity, width), BF),
            pltpu.VMEM((slot_count, shard_count * capacity), I32),
            pltpu.SMEM((slot_count, shard_count * capacity), I32),
            dma,
            dma((slot_count,)),
            dma((slot_count,)),
        ],
        compiler_params=params(50),
        cost_estimate=pl.CostEstimate(flops=12 * 10**9, bytes_accessed=4 * 2**20, transcendentals=2**24),
        name="attend",
    )(lengths, received, head_cache)

    answered, weight_three, weight_four, queries = lax.optimization_barrier(
        (answered, weight_three, weight_four, queries)
    )
    weight_five = swap(weight_three, "tensor", tensor_count // 8)
    returned = lax.all_to_all(
        answered.reshape(shard_count, slot_count * capacity, width), "shard", split_axis=0, concat_axis=0, tiled=True
    ).reshape(positions, width)

    returned, weight_five = lax.optimization_barrier((returned, weight_five))
    own_weights = (weight_two, weight_three, weight_four, weight_five)
    other_weights = [swap(part, "shard", 1) for part in own_weights]
    block = 512
    gate_and_self = pl.pallas_call(
        side_kernel,
        grid=(row_count // block,),
        in_specs=[
            pl.BlockSpec((block, model_width), lambda i: (i, 0)),
            pl.BlockSpec((model_width * PARTS, width), lambda i: (0, 0)),
            pl.BlockSpec((block, width), lambda i: (i, 0)),
            SCALARS,
        ],
        out_specs=pl.BlockSpec((block, 2 * width), lambda i: (i, 0)),
        out_shape=jax.ShapeDtypeStruct((row_count, 2 * width), F32),
        scratch_shapes=[
            pltpu.VMEM((model_width * PARTS, width), F32),
            pltpu.VMEM((model_width, (PARTS - 1) * width), BF),
        ],
        compiler_params=params(32),
        cost_estimate=pl.CostEstimate(flops=4 * 10**9, bytes_accessed=6 * 2**20, transcendentals=2**20),
        name="side",
    )(cand_rows, weights, queries, self_bias)

    owned = row_count // tensor_count
    place = (2 * my_tensor + core).reshape(1).astype(I32)
    residual = lax.dynamic_slice_in_dim(cand_rows, my_tensor * owned, owned, 0)

    hidden = pl.pallas_call(
        hidden_kernel,
        in_specs=[SCALARS, WHOLE, ANY],
        out_specs=WHOLE,
        out_shape=jax.ShapeDtypeStruct((row_count, width), BF),
        scratch_shapes=[
            pltpu.VMEM((row_count, 2 * width), F32),
            pltpu.VMEM((positions, width), F32),
            pltpu.VMEM((row_count, width), F32),
            dma,
        ],
        compiler_params=params(58),
        cost_estimate=pl.CostEstimate(flops=4 * 10**9, bytes_accessed=4 * 2**20, transcendentals=2**18),
        name="hidden",
    )(places.reshape(row_count), returned, gate_and_self)

    gathered = lax.all_to_all(
        hidden.reshape(tensor_count, owned, width), "tensor", split_axis=0, concat_axis=0, tiled=True
    )
    out_width = model_width // tensor_count
    mixed = pl.pallas_call(
        output_kernel,
        in_specs=[SCALARS] + [WHOLE] * 10,
        out_specs=WHOLE,
        out_shape=jax.ShapeDtypeStruct((tensor_count, owned, out_width), BF),
        compiler_params=params(24),
        cost_estimate=pl.CostEstimate(flops=10**9, bytes_accessed=4 * 2**20, transcendentals=0),
        name="output",
    )(place, gathered, residual, *own_weights, *other_weights)
    placed = lax.all_to_all(mixed, "tensor", split_axis=0, concat_axis=0, tiled=True)
    return placed.reshape(row_count, out_width)


def solution(mesh):
    in_specs = (
        P("shard", None),
        P(None, None, "tensor"),
        P("tensor", None),
        P("tensor"),
        P("shard", None, None, "tensor"),
        P(),
        P("shard", None),
        P(),
    )
    out_specs = P("shard", "tensor")
    return jax.shard_map(body, mesh=mesh, in_specs=in_specs, out_specs=out_specs, check_vma=False)
```

```python
import functools

import jax
import jax.numpy as jnp
from jax import lax
from jax.experimental import pallas as pl
from jax.experimental.pallas import tpu as pltpu
from jax.sharding import PartitionSpec as P

DH = 64
epsilon = 1e-06
BF = jnp.bfloat16
F32 = jnp.float32
I32 = jnp.int32
PARTS = 4
QUERY = 2
CHUNK = 1024
NORMED = 512
RANKED = 256
ROWS = 256
TILE = 16
KBLK = 512
BATCH = 128
MARK = 2.0**20
MIB = 1024 * 1024


def dot(a, b):
    return jnp.dot(a, b, preferred_element_type=F32)


def inverse_rms(rows):
    wide = rows.astype(F32)
    return lax.rsqrt(jnp.mean(wide * wide, axis=1, keepdims=True) + epsilon)


def silu(x):
    half = 0.5 * x
    return half + half * jnp.tanh(half)


def query_kernel(
    capacity, slot_count, cand_ref, weight_ref, slot_ref, hot_ref, sent_ref, query_ref, place_ref,
    rows, raw, wide, weight, places, queries, sent, packed, row_sem, raw_sem, place_sem, out_sem,
):
    row_count, model_width = rows.shape
    shard_count = hot_ref.shape[1]
    slot_total = shard_count * slot_count
    chunks = row_count // CHUNK
    raw_copy = pltpu.make_async_copy(weight_ref, raw, raw_sem)
    raw_copy.start()
    row_copies = []
    for i in range(chunks):
        part = pl.ds(i * CHUNK, CHUNK)
        row_copies.append(pltpu.make_async_copy(cand_ref.at[part], rows.at[part], row_sem.at[i]))
        row_copies[i].start()

    before = lax.broadcasted_iota(I32, (RANKED, RANKED), 0) <= lax.broadcasted_iota(I32, (RANKED, RANKED), 1)
    before = before.astype(F32).astype(BF)
    slots = lax.broadcasted_iota(I32, (8, slot_total), 1)
    other = (slots // slot_count) ^ (shard_count // 2)
    hot = jnp.broadcast_to(hot_ref[...].astype(F32), (8, shard_count)).astype(BF)
    shard = lax.broadcasted_iota(I32, (shard_count, slot_total), 0)
    owner = lax.broadcasted_iota(I32, (shard_count, slot_total), 1) // slot_count
    own_hot = dot(hot, (shard == owner).astype(F32).astype(BF)).astype(I32)
    other_hot = dot(hot, (shard == owner ^ (shard_count // 2)).astype(F32).astype(BF)).astype(I32)
    source = jnp.where(slots % slot_count == own_hot, other * slot_count + other_hot, slots).astype(F32).astype(BF)
    carry = jnp.zeros((slot_total, 1), F32)
    for i in range(row_count // RANKED):
        part = slice(i * RANKED, (i + 1) * RANKED)
        member = (slot_ref[:, part] == lax.broadcasted_iota(I32, (slot_total, RANKED), 0)).astype(F32)
        narrow = member.astype(BF)
        counted = dot(narrow, before) + carry
        carry = counted[:, RANKED - 1 :]
        base = dot(source, narrow)[:1]
        rank = jnp.sum(member * counted, axis=0, keepdims=True) - 1.0
        place_ref[:, part] = (base * capacity + rank).astype(I32)
    place_copy = pltpu.make_async_copy(place_ref, places, place_sem)
    place_copy.start()

    sent[...] = jnp.full(sent.shape, MARK, F32)
    raw_copy.wait()
    wide[...] = raw[...].astype(F32)
    weight[...] = wide[pl.ds(QUERY, model_width, stride=PARTS), :].astype(BF)
    for i in range(chunks):
        part = pl.ds(i * CHUNK, CHUNK)
        row_copies[i].wait()
        block = rows[part, :]
        query = silu(dot(block, weight[...]) * inverse_rms(block)).astype(BF) * BF(0.5 * DH**-0.5)
        query_ref[part, :] = query
        queries[part, :] = query.astype(F32)
    place_copy.wait()

    @pl.loop(0, row_count // BATCH)
    def _(i):
        start = pl.multiple_of(i * BATCH, BATCH)
        for j in range(BATCH):
            sent[pl.ds(places[0, start + j], 1), :] = queries[pl.ds(start + j, 1), :]

    out_copies = []
    quarter = sent.shape[0] // 4
    for i in range(4):
        part = pl.ds(i * quarter, quarter)
        packed[part, :] = sent[part, :].astype(BF)
        out_copies.append(pltpu.make_async_copy(packed.at[part], sent_ref.at[part], out_sem.at[i]))
        out_copies[i].start()
    for copy in out_copies:
        copy.wait()


def side_kernel(cand_ref, weight_ref, query_ref, bias_ref, pair_ref, wide, weight):
    width = pair_ref.shape[1] // 2
    model_width = cand_ref.shape[1]

    @pl.when(pl.program_id(0) == 0)
    def _():
        wide[...] = weight_ref[...].astype(F32)
        for i, part in enumerate((0, 1, 3)):
            weight[:, i * width : (i + 1) * width] = wide[pl.ds(part, model_width, stride=PARTS), :].astype(BF)

    rows = cand_ref[...]
    parts = silu(dot(rows, weight[...]) * inverse_rms(rows)).astype(BF)
    pair_ref[:, :width] = parts[:, :width].astype(F32)
    value = parts[:, width : 2 * width].astype(F32)
    product = query_ref[...].astype(F32) * parts[:, 2 * width :].astype(F32)
    lane = lax.broadcasted_iota(I32, product.shape, 1)
    score = jnp.zeros_like(product)
    for head in range(width // DH):
        here = lane // DH == head
        total = jnp.sum(jnp.where(here, product, 0.0), axis=1, keepdims=True)
        score = jnp.where(here, 2.0 * total + bias_ref[head], score)
    pair_ref[:, width:] = silu(score) * value


def history_kernel(length_ref, cache_ref, out_ref, wide):
    slot_count, total, width = cache_ref.shape
    heads = width // DH
    history = total // 2
    value_lane = lax.broadcasted_iota(I32, (KBLK, width), 1)
    key_row = lax.broadcasted_iota(I32, (width, KBLK), 0)
    for slot in range(slot_count):
        length = length_ref[slot]
        wide[...] = cache_ref[slot].astype(F32)
        for block in range(history // KBLK):
            keys = wide[pl.ds(2 * block * KBLK, KBLK, stride=2), :].T
            values = wide[pl.ds(2 * block * KBLK + 1, KBLK, stride=2), :]
            live = block * KBLK + lax.broadcasted_iota(I32, (KBLK, width), 0) < length
            for head in range(heads):
                start = (block * heads + head) * KBLK
                out_ref[slot, 0, start : start + KBLK, :] = jnp.where(
                    live & (value_lane // DH == head), values, 0.0
                ).astype(BF)
                part = jnp.where(key_row // DH == head, keys, 0.0).astype(BF)
                for i in range(KBLK // width):
                    place = slice(start + i * width, start + (i + 1) * width)
                    out_ref[slot, 1, place, :] = part[:, i * width : (i + 1) * width]


def attend_kernel(
    length_ref, packet_ref, cache_hbm, answer_ref,
    cache_ref, packed, totals, answers, flag_rows, flags, flag_sem, in_sem, out_sem,
):
    shard_count, slot_count, item_count, width = packet_ref.shape
    heads = width // DH
    per = item_count // TILE
    together = 8
    history = cache_ref.shape[2] // heads
    ones = jnp.ones((8, width), BF)
    in_copies = []
    for slot in range(slot_count):
        in_copies.append(pltpu.make_async_copy(cache_hbm.at[slot], cache_ref.at[slot], in_sem.at[slot]))
    for copy in in_copies:
        copy.start()
    for slot in range(slot_count):
        rows = packet_ref[:, slot].reshape(shard_count * item_count, width)
        sums = lax.dot_general(ones, rows, (((1,), (1,)), ((), ())), preferred_element_type=F32)
        flag_rows[slot : slot + 1, :] = jnp.where(sums[:1] < MARK, TILE, 0).astype(I32)
    flag_copy = pltpu.make_async_copy(flag_rows, flags, flag_sem)
    flag_copy.start()
    flag_copy.wait()
    out_copies = []
    for slot in range(slot_count):
        blocks = (length_ref[slot] + KBLK - 1) // KBLK

        def pack(i, offset):
            tiles = [
                packet_ref[i * together + j, slot, k * TILE : (k + 1) * TILE, :]
                for j in range(together)
                for k in range(per)
            ]
            for j, tile in enumerate(tiles):
                packed[pl.ds(pl.multiple_of(offset, TILE), TILE), :] = tile
                offset = offset + flags[slot, (i * together * per + j) * TILE]
            return offset

        total_rows = lax.fori_loop(0, shard_count // together, pack, jnp.int32(0))
        row_blocks = (total_rows + ROWS // 2 - 1) // ROWS
        in_copies[slot].wait()

        def attend_rows(start, count, blocks_here):
            rows = packed[pl.ds(start, count), :]

            def score(j):
                parts = [
                    cache_ref[slot, 1, j * KBLK + i * width : j * KBLK + (i + 1) * width, :]
                    for i in range(KBLK // width)
                ]
                return dot(rows, jnp.concatenate(parts, axis=1))

            total = jnp.zeros((count, width), F32)
            half = score(0)
            for j in range(heads * blocks_here):
                later = score(j + 1) if j + 1 < heads * blocks_here else None
                weights = (half + half * jnp.tanh(half)).astype(BF)
                total = total + dot(weights, cache_ref[slot, 0, j * KBLK : (j + 1) * KBLK, :])
                half = later
            totals[pl.ds(start, count), :] = total.astype(BF)

        for k in range(1, history // KBLK + 1):

            @pl.when(blocks == k)
            def _():
                @pl.loop(0, row_blocks)
                def _(part):
                    attend_rows(pl.multiple_of(part * ROWS, ROWS), ROWS, k)

                @pl.when(total_rows > row_blocks * ROWS)
                def _():
                    attend_rows(pl.multiple_of(row_blocks * ROWS, ROWS), ROWS // 2, k)

        def unpack(i, offset):
            tiles = []
            for j in range(together * per):
                tiles.append(totals[pl.ds(pl.multiple_of(offset, TILE), TILE), :])
                offset = offset + flags[slot, (i * together * per + j) * TILE]
            for j in range(together):
                for k in range(per):
                    answers[slot, i * together + j, k * TILE : (k + 1) * TILE, :] = tiles[j * per + k]
            return offset

        lax.fori_loop(0, shard_count // together, unpack, jnp.int32(0))
        out_copies.append(pltpu.make_async_copy(answers.at[slot], answer_ref.at[:, slot], out_sem.at[slot]))
        out_copies[slot].start()
    for copy in out_copies:
        copy.wait()


def hidden_kernel(place_ref, returned_ref, pair_hbm, hidden_ref, pair_ref, wide, chosen, pair_sem):
    row_count, width = chosen.shape
    pair_copy = pltpu.make_async_copy(pair_hbm, pair_ref, pair_sem)
    pair_copy.start()
    wide[...] = returned_ref[...].astype(F32)

    @pl.loop(0, row_count // BATCH)
    def _(i):
        start = pl.multiple_of(i * BATCH, BATCH)
        for j in range(BATCH):
            chosen[pl.ds(start + j, 1), :] = wide[pl.ds(place_ref[start + j], 1), :]

    pair_copy.wait()
    same = lax.broadcasted_iota(I32, (width, width), 0) // DH == lax.broadcasted_iota(I32, (width, width), 1) // DH
    ones = same.astype(F32).astype(BF)
    for i in range(row_count // NORMED):
        part = pl.ds(i * NORMED, NORMED)
        attention = chosen[part, :] + pair_ref[part, width:]
        square = attention * attention
        high = square.astype(BF)
        low = (square - high.astype(F32)).astype(BF)
        mean = (dot(high, ones) + dot(low, ones)) * (1.0 / DH)
        hidden_ref[part, :] = (attention * lax.rsqrt(mean + epsilon) * pair_ref[part, :width]).astype(BF)


def output_kernel(
    place_ref, hidden_ref, residual_ref, own_0, own_1, own_2, own_3, other_0, other_1, other_2, other_3, out_ref
):
    count, owned, width = hidden_ref.shape
    place = lax.div(place_ref[0], 2)
    core = lax.rem(place_ref[0], 2)
    order = [flip ^ i for i in range(2) for flip in (0, 4, 2, 6)]
    hidden = jnp.concatenate([hidden_ref[place ^ flip] for flip in order], axis=1)
    part = out_ref.shape[2]
    half_width = own_0.shape[2]
    products = []
    for half, refs in ((core, (own_0, own_1, own_2, own_3)), (1 - core, (other_0, other_1, other_2, other_3))):
        product = residual_ref[:, pl.ds(pl.multiple_of(half * half_width, half_width), half_width)].astype(F32)
        for i, ref in enumerate(refs):
            deep = hidden.shape[1] // len(refs)
            product = product + dot(hidden[:, i * deep : (i + 1) * deep], ref[...].reshape(deep, half_width))
        products.append((half, product))
    for half, product in products:
        mixed = product.astype(BF)
        for i in range(half_width // part):
            out_ref[half * (half_width // part) + i] = mixed[:, i * part : (i + 1) * part]


def params(limit):
    return pltpu.CompilerParams(vmem_limit_bytes=limit * MIB)


ANY = pl.BlockSpec(memory_space=pl.ANY)
WHOLE = pl.BlockSpec(memory_space=pltpu.VMEM)
SCALARS = pl.BlockSpec(memory_space=pltpu.SMEM)


def body(cand_rows, proj_weight, out_weight, self_bias, history_cache, history_length, candidate_slot, hot_slot):
    shard_count = lax.axis_size("shard")
    my_shard = lax.axis_index("shard")
    tensor_count = lax.axis_size("tensor")
    my_tensor = lax.axis_index("tensor")
    row_count, model_width = cand_rows.shape
    width = out_weight.shape[0]
    heads = width // DH
    slot_count = history_cache.shape[0]
    slot_total = shard_count * slot_count
    capacity = 2 * row_count // slot_total
    history = history_cache.shape[1]
    positions = slot_total * capacity
    dma = pltpu.SemaphoreType.DMA

    core = my_shard % 2
    half_width = model_width // 2
    weight_half = lax.dynamic_slice_in_dim(out_weight, core * half_width, half_width, 1)[None]

    def swap(array, axis, distance):
        return lax.ppermute(array, axis, [(i, i ^ distance) for i in range(lax.axis_size(axis))])

    weights = proj_weight.reshape(model_width * PARTS, width)
    slot_row = candidate_slot.reshape(1, row_count)
    sent, queries, places = pl.pallas_call(
        functools.partial(query_kernel, capacity, slot_count),
        in_specs=[ANY, ANY, WHOLE, WHOLE],
        out_specs=[ANY, WHOLE, WHOLE],
        out_shape=[
            jax.ShapeDtypeStruct((positions, width), BF),
            jax.ShapeDtypeStruct((row_count, width), BF),
            jax.ShapeDtypeStruct((1, row_count), I32),
        ],
        scratch_shapes=[
            pltpu.VMEM((row_count, model_width), BF),
            pltpu.VMEM((model_width * PARTS, width), BF),
            pltpu.VMEM((model_width * PARTS, width), F32),
            pltpu.VMEM((model_width, width), BF),
            pltpu.SMEM((1, row_count), I32),
            pltpu.VMEM((row_count, width), F32),
            pltpu.VMEM((positions, width), F32),
            pltpu.VMEM((positions, width), BF),
            dma((row_count // CHUNK,)),
            dma,
            dma,
            dma((4,)),
        ],
        compiler_params=params(60),
        cost_estimate=pl.CostEstimate(flops=4 * 10**9, bytes_accessed=6 * 2**20, transcendentals=2**18),
        name="query",
    )(cand_rows, weights, slot_row, hot_slot.reshape(1, shard_count))

    sent, weight_half = lax.optimization_barrier((sent, weight_half))
    weight_one = swap(weight_half, "tensor", tensor_count // 2)
    received = lax.all_to_all(
        sent.reshape(shard_count, slot_count * capacity, width), "shard", split_axis=0, concat_axis=0, tiled=True
    ).reshape(shard_count, slot_count, capacity, width)

    lengths = lax.dynamic_slice_in_dim(history_length, my_shard * slot_count, slot_count)
    head_cache = pl.pallas_call(
        history_kernel,
        grid=(1,),
        in_specs=[SCALARS, pl.BlockSpec((slot_count, 2 * history, width), lambda i: (0, 0, 0))],
        out_specs=pl.BlockSpec((slot_count, 2, heads * history, width), lambda i: (0, 0, 0, 0)),
        out_shape=jax.ShapeDtypeStruct((slot_count, 2, heads * history, width), BF),
        scratch_shapes=[pltpu.VMEM((2 * history, width), F32)],
        compiler_params=params(60),
        cost_estimate=pl.CostEstimate(flops=10**9, bytes_accessed=6 * 2**20, transcendentals=0),
        name="history",
    )(lengths, history_cache.reshape(slot_count, 2 * history, width))

    weight_two = jnp.concatenate([weight_half, weight_one], axis=0)
    weight_three = swap(weight_two, "tensor", tensor_count // 4)
    weight_four = swap(weight_two, "tensor", tensor_count // 8)
    answered = pl.pallas_call(
        attend_kernel,
        in_specs=[SCALARS, WHOLE, ANY],
        out_specs=ANY,
        out_shape=jax.ShapeDtypeStruct(received.shape, BF),
        scratch_shapes=[
            pltpu.VMEM(head_cache.shape, BF),
            pltpu.VMEM((shard_count * capacity + ROWS, width), BF),
            pltpu.VMEM((shard_count * capacity + ROWS, width), BF),
            pltpu.VMEM((slot_count, shard_count, capacity, width), BF),
            pltpu.VMEM((slot_count, shard_count * capacity), I32),
            pltpu.SMEM((slot_count, shard_count * capacity), I32),
            dma,
            dma((slot_count,)),
            dma((slot_count,)),
        ],
        compiler_params=params(50),
        cost_estimate=pl.CostEstimate(flops=12 * 10**9, bytes_accessed=4 * 2**20, transcendentals=2**24),
        name="attend",
    )(lengths, received, head_cache)

    answered, weight_three, weight_four, queries = lax.optimization_barrier(
        (answered, weight_three, weight_four, queries)
    )
    weight_five = swap(weight_three, "tensor", tensor_count // 8)
    returned = lax.all_to_all(
        answered.reshape(shard_count, slot_count * capacity, width), "shard", split_axis=0, concat_axis=0, tiled=True
    ).reshape(positions, width)

    returned, weight_five = lax.optimization_barrier((returned, weight_five))
    own_weights = (weight_two, weight_three, weight_four, weight_five)
    other_weights = [swap(part, "shard", 1) for part in own_weights]
    block = 512
    gate_and_self = pl.pallas_call(
        side_kernel,
        grid=(row_count // block,),
        in_specs=[
            pl.BlockSpec((block, model_width), lambda i: (i, 0)),
            pl.BlockSpec((model_width * PARTS, width), lambda i: (0, 0)),
            pl.BlockSpec((block, width), lambda i: (i, 0)),
            SCALARS,
        ],
        out_specs=pl.BlockSpec((block, 2 * width), lambda i: (i, 0)),
        out_shape=jax.ShapeDtypeStruct((row_count, 2 * width), F32),
        scratch_shapes=[
            pltpu.VMEM((model_width * PARTS, width), F32),
            pltpu.VMEM((model_width, (PARTS - 1) * width), BF),
        ],
        compiler_params=params(32),
        cost_estimate=pl.CostEstimate(flops=4 * 10**9, bytes_accessed=6 * 2**20, transcendentals=2**20),
        name="side",
    )(cand_rows, weights, queries, self_bias)

    owned = row_count // tensor_count
    place = (2 * my_tensor + core).reshape(1).astype(I32)
    residual = lax.dynamic_slice_in_dim(cand_rows, my_tensor * owned, owned, 0)

    hidden = pl.pallas_call(
        hidden_kernel,
        in_specs=[SCALARS, WHOLE, ANY],
        out_specs=WHOLE,
        out_shape=jax.ShapeDtypeStruct((row_count, width), BF),
        scratch_shapes=[
            pltpu.VMEM((row_count, 2 * width), F32),
            pltpu.VMEM((positions, width), F32),
            pltpu.VMEM((row_count, width), F32),
            dma,
        ],
        compiler_params=params(58),
        cost_estimate=pl.CostEstimate(flops=4 * 10**9, bytes_accessed=4 * 2**20, transcendentals=2**18),
        name="hidden",
    )(places.reshape(row_count), returned, gate_and_self)

    gathered = lax.all_to_all(
        hidden.reshape(tensor_count, owned, width), "tensor", split_axis=0, concat_axis=0, tiled=True
    )
    out_width = model_width // tensor_count
    mixed = pl.pallas_call(
        output_kernel,
        in_specs=[SCALARS] + [WHOLE] * 10,
        out_specs=WHOLE,
        out_shape=jax.ShapeDtypeStruct((tensor_count, owned, out_width), BF),
        compiler_params=params(24),
        cost_estimate=pl.CostEstimate(flops=10**9, bytes_accessed=4 * 2**20, transcendentals=0),
        name="output",
    )(place, gathered, residual, *own_weights, *other_weights)
    placed = lax.all_to_all(mixed, "tensor", split_axis=0, concat_axis=0, tiled=True)
    return placed.reshape(row_count, out_width)


def solution(mesh):
    in_specs = (
        P("shard", None),
        P(None, None, "tensor"),
        P("tensor", None),
        P("tensor"),
        P("shard", None, None, "tensor"),
        P(),
        P("shard", None),
        P(),
    )
    out_specs = P("shard", "tensor")
    return jax.shard_map(body, mesh=mesh, in_specs=in_specs, out_specs=out_specs, check_vma=False)
```
